512 devices in a mesh: energy: 8 (over x, core), space: 64 (over y, z).
Axes of the slice: x: 4, y: 8, z: 8, core: 2. Of those that a mesh axis runs over, the one named last changes fastest.
Arguments:
- green_blocks: bfloat16 [16, 64, 256, 256], P('energy', 'space'), as said below
- energy_weights: float32 [16], P('energy'), may hold values from 0.00625 to 0.0625
- basis: bfloat16 [64, 256, 64, 256], P('space', None, 'energy'), may hold values from -0.75 to 0.75
- block_layer: int32 [64], P('space'), may hold values from 0 to 255, as said below
- potential_in: float32 [256, 64, 256], P('space', 'energy'), may hold values from -6 to 6
- doping: float32 [256, 64, 256], P('space', 'energy'), may hold values from -12 to 12
Outputs:
- potential: float32 [256, 64, 256], P('space', 'energy')
- residual: float32 [256, 64, 256], P('space', 'energy')
- onsite: float32 [64, 256], P('space')
The draws below stay inside these ranges and needn't reach their ends.
Inputs may be any that keep to these rules, and one draw needn't show every extreme that they name: `green_blocks`: each block G[e, b] is symmetric positive definite. `block_layer`: block b lies in the slab of the space index that holds it or in the next slab: its layer is at least (b) * 4 and under (b + 2) * 4; the first block takes layer 0 and the last takes layer 255.
All inputs are finite; a program needn't handle non-finite values.
Results may differ from the reference program's by a relative error of at most 0.0035.
Values may be sent and summed in bfloat16 or wider, within the bound.
No kernel may reach another device: no remote copies, remote signals or barrier semaphores. Data moves between devices by JAX's collectives and lax.ppermute only.
A program may use at most 64 MiB of HBM per device.

```python
import math
import jax
import jax.numpy as jnp
from jax import lax

BS = 256
NB_DEV = 1
CX = 4
CZ = 256
ITERS = 3
NX = 256
NY = 64
ENERGIES = 16
NB = 64


def draw_green_blocks(key, part):
    key = jax.random.fold_in(key, 3)
    key_place, key_sign, key_mag, key_diag = jax.random.split(key, 4)
    spread = BS / 8.0
    places = jax.random.uniform(key_place, (NB, BS), jnp.float32, 0.0, spread)
    signs = (2 * jax.random.randint(key_sign, (NB, BS), 0, 2, dtype=jnp.int32) - 1).astype(jnp.float32)
    magnitude = jax.random.uniform(key_mag, (ENERGIES, NB, BS), jnp.float32, 0.5, 1.5)
    diag = jax.random.uniform(key_diag, (ENERGIES, NB, BS), jnp.float32, 0.2, 0.5)
    amplitude = signs[None, :, :] * magnitude
    kernel = jnp.exp(-jnp.abs(places[:, :, None] - places[:, None, :]))
    paired = amplitude[..., :, None] * amplitude[..., None, :]
    order = jnp.arange(BS)
    unit = order[:, None] == order[None, :]
    full = 2.0 * paired * kernel[None] + jnp.where(unit, diag[..., None], 0.0)
    return full.astype(jnp.bfloat16)


def draw_block_layer(key, part):
    key = jax.random.fold_in(key, 7)
    index = jnp.arange(NB, dtype=jnp.int32)
    holder = index // NB_DEV
    start = holder * CX
    reach = jnp.minimum(2 * CX, NX - start)
    offset = jax.random.randint(key, (NB,), 0, reach, dtype=jnp.int32)
    layer = start + offset
    layer = jnp.where(index == 0, 0, layer)
    layer = jnp.where(index == NB - 1, NX - 1, layer)
    return layer.astype(jnp.int32)


def shard_levels(stream_key, dims, cuts, low, top_value):
    gain, own = 1.0, jax.random.fold_in(stream_key, 6)
    for dim, blocks in cuts:
        heights = jnp.exp(jax.random.uniform(jax.random.fold_in(own, dim), (blocks,), jnp.float32, low / len(cuts), top_value / len(cuts)))
        gain = gain * jnp.repeat(heights, dims[dim] // blocks).reshape([-1 if axis == dim else 1 for axis in range(len(dims))])
    return gain


def noise(key, shape, deviation, most, cuts=(), kind=jnp.bfloat16):
    level = shard_levels(key, shape, cuts, -0.22, 0.18) if cuts else 1.0
    values = jax.random.normal(key, shape, jnp.float32) * deviation * level
    return jnp.minimum(jnp.maximum(values, -most), most).astype(kind)


def setup_inputs(seed: int = 0) -> dict:
    key_of = jax.random.split(jax.random.key(seed), 7)
    green_blocks = draw_green_blocks(jax.random.fold_in(key_of[6], 71), 0)
    energy_weights = jnp.clip(jnp.exp(math.log(0.0625) - 2.3025851 * jax.random.uniform(key_of[1], (ENERGIES,), jnp.float32) ** shard_levels(key_of[1], (ENERGIES,), ((0, 8),), -0.2, 0.2)), 0.00625, 0.0625)
    basis = noise(key_of[2], (NB, BS, NY, CZ), 0.125, 0.75, ((0, 64), (2, 8)))
    block_layer = draw_block_layer(jax.random.fold_in(key_of[6], 71), 0)
    potential_in = noise(key_of[4], (NX, NY, CZ), 1.0, 6.0, ((0, 64), (1, 8)), jnp.float32)
    doping = noise(key_of[5], (NX, NY, CZ), 2.0, 12.0, ((0, 64), (1, 8)), jnp.float32)
    return {"green_blocks": green_blocks, "energy_weights": energy_weights, "basis": basis, "block_layer": block_layer, "potential_in": potential_in, "doping": doping}


def operate(field, mass):
    padded = jnp.pad(field, 1)
    beside = padded[2:, 1:-1, 1:-1] + padded[:-2, 1:-1, 1:-1]
    beside = beside + padded[1:-1, 2:, 1:-1] + padded[1:-1, :-2, 1:-1]
    beside = beside + padded[1:-1, 1:-1, 2:] + padded[1:-1, 1:-1, :-2]
    return (6.0 + mass) * field - beside


def reference(green_blocks, energy_weights, basis, block_layer, potential_in, doping):
    def project(items):
        blocks, functions = items
        density = jnp.einsum("e,eij->ij", energy_weights, blocks.astype(jnp.float32), precision=lax.Precision.HIGHEST).astype(jnp.bfloat16)
        flat = functions.reshape(BS, NY * CZ)
        applied = jnp.dot(density, flat, preferred_element_type=jnp.float32)
        return jnp.sum(flat.astype(jnp.float32) * applied, axis=0)

    charge_blocks = lax.map(project, (jnp.swapaxes(green_blocks, 0, 1), basis))
    charge = jax.ops.segment_sum(charge_blocks, block_layer, NX).reshape(NX, NY, CZ)
    mass = charge / 4.0
    inverse = 1.0 / (6.0 + mass)
    rhs = doping - charge - operate(potential_in, jnp.zeros_like(mass))
    update = jnp.zeros_like(rhs)
    residual = rhs
    precond = inverse * residual
    direction = precond
    norm_now = jnp.sum(residual * precond)
    for step in range(ITERS):
        image = operate(direction, mass)
        alpha = norm_now / jnp.sum(direction * image)
        update = update + alpha * direction
        residual = residual - alpha * image
        precond = inverse * residual
        norm_next = jnp.sum(residual * precond)
        direction = precond + (norm_next / norm_now) * direction
        norm_now = norm_next
    potential = potential_in + update
    on_layer = potential.reshape(NX, NY * CZ)[block_layer]

    def onsite_one(items):
        functions, values = items
        flat = functions.reshape(BS, NY * CZ).astype(jnp.float32)
        return jnp.sum(flat * flat * values[None, :], axis=1)

    onsite = lax.map(onsite_one, (basis, on_layer))
    return potential, residual, onsite
```

```python
import jax
import jax.numpy as jnp
from jax import lax
from jax.sharding import PartitionSpec as P

ITERS = 3
HALO = 3
F32 = jnp.float32
BF16 = jnp.bfloat16


def moved(value, axis, by):
    count = lax.axis_size(axis)
    pairs = [(i, i + by) for i in range(count) if 0 <= i + by < count]
    return lax.ppermute(value, axis, pairs)


def summed(value, axis):
    count = lax.axis_size(axis)
    copies = jnp.broadcast_to(value[None], (count,) + value.shape)
    return jnp.sum(lax.all_to_all(copies, axis, 0, 0).astype(F32), axis=0)


def along_z(field):
    zero = jnp.zeros_like(field[..., :1])
    up = jnp.concatenate([field[..., 1:], zero], axis=-1)
    down = jnp.concatenate([zero, field[..., :-1]], axis=-1)
    return up + down


def neighbours(field):
    inner = field[1:-1]
    rows = jnp.roll(inner, 1, axis=1) + jnp.roll(inner, -1, axis=1)
    return field[:-2] + field[2:] + rows + along_z(inner)


def neighbours_in_block(field):
    total = along_z(field)
    for dim in (0, 1):
        width = [(0, 0)] * 3
        width[dim] = (1, 1)
        padded = jnp.pad(field, width)
        count = field.shape[dim]
        total = total + lax.slice_in_dim(padded, 0, count, axis=dim)
        total = total + lax.slice_in_dim(padded, 2, count + 2, axis=dim)
    return total


def packed_density(green, weights):
    total = sum(weights[e] * green[e, 0].astype(F32) for e in range(green.shape[0]))
    half = total.shape[0] // 2
    row = lax.broadcasted_iota(jnp.int32, (half, half), 0)
    col = lax.broadcasted_iota(jnp.int32, (half, half), 1)
    low = total[half:, half:]
    mixed = jnp.where(row <= col, total[:half, :half], low)
    diagonal = jnp.sum(jnp.where(row == col, low, 0.0), axis=0)
    tail = jnp.broadcast_to(diagonal[None], (16, half))
    return jnp.concatenate([total[:half, half:], mixed, tail], axis=0).astype(BF16)


def unpacked_density(packed):
    half = packed.shape[1]
    packed = packed.astype(BF16).astype(F32)
    row = lax.broadcasted_iota(jnp.int32, (half, half), 0)
    col = lax.broadcasted_iota(jnp.int32, (half, half), 1)
    cross, mixed = packed[:half], packed[half : 2 * half]
    first = jnp.where(row < col, 2.0 * mixed, jnp.where(row == col, mixed, 0.0))
    last = jnp.where(row > col, 2.0 * mixed, 0.0)
    last = last + jnp.where(row == col, packed[2 * half][None], 0.0)
    top = jnp.concatenate([first, 2.0 * cross], axis=1)
    bottom = jnp.concatenate([jnp.zeros_like(last), last], axis=1)
    return jnp.concatenate([top, bottom], axis=0).astype(BF16)


def coefficients(m):
    def inner(a, b, low=0):
        return sum(
            x * y * (m[i + j] - m[i + j + 1] if low else m[i + j])
            for i, x in enumerate(a)
            for j, y in enumerate(b)
        )

    z, d, u, norm = [1.0], [1.0], [], m[0]
    for step in range(ITERS):
        alpha = norm / inner(d, d, 1)
        u = [a + alpha * b for a, b in zip(u + [0.0], d)]
        shifted = [0.0] + d
        z = [a - alpha * (b - c) for a, b, c in zip(z + [0.0], d + [0.0], shifted)]
        if step < ITERS - 1:
            after = inner(z, z)
            d = [a + after / norm * b for a, b in zip(z, d + [0.0])]
            norm = after
    return u, z


def shards(green, weights, basis, block_layer, pot, dop):
    layers, rows, depth = pot.shape
    e, s = lax.axis_index("energy"), lax.axis_index("space")
    ne, ns = lax.axis_size("energy"), lax.axis_size("space")
    functions = basis[0]

    density = unpacked_density(summed(packed_density(green, weights), "energy"))
    applied = jnp.einsum("ij,jyz->iyz", density, functions, preferred_element_type=F32)
    charge_block = jnp.sum(functions * applied, axis=0)

    base = dop - 6.0 * pot + neighbours_in_block(pot)
    fields = jnp.concatenate([base, pot, charge_block[None]], axis=0)
    above = moved(fields[:, :4], "energy", -1)
    below = moved(fields[:, -4:], "energy", 1)
    fields = jnp.concatenate([fields, above, below], axis=1)
    wide = fields.shape[1]
    line = lax.broadcasted_iota(jnp.int32, (1, wide, depth), 1)
    wide_pot = fields[layers : 2 * layers]
    ahead = jnp.roll(wide_pot, 1, axis=1)
    behind = jnp.roll(wide_pot, -1, axis=1)
    wide_base = fields[:layers]
    wide_base = wide_base + jnp.where((line == rows) | (line == 0), ahead, 0.0)
    wide_base = wide_base + jnp.where((line == rows - 1) | (line == wide - 1), behind, 0.0)
    number = block_layer[0].astype(F32)
    line_of_layer = rows + HALO
    charge_block = jnp.where(line[0] == line_of_layer, number, fields[2 * layers])

    up = jnp.concatenate([wide_base[1:], wide_pot[-1:], charge_block[None]], axis=0)
    down = jnp.concatenate([wide_base[:HALO], wide_pot[:1], charge_block[None]], axis=0)
    low = moved(up, "space", 1)
    high = moved(down, "space", -1)
    lowest = moved(charge_block, "space", 2)

    zero = jnp.zeros_like(wide_pot[:1])
    two = jnp.concatenate([zero, zero], axis=0)
    whole = jnp.concatenate([low[:HALO], wide_base, high[:HALO]], axis=0)
    seam = jnp.concatenate(
        [two, wide_pot[:1], low[HALO : HALO + 1], two, high[HALO : HALO + 1], wide_pot[-1:], two], axis=0
    )
    blocks = [lowest, low[HALO + 1], charge_block, high[HALO + 1]]
    first = (s * layers - HALO).astype(F32)
    layer = first + lax.broadcasted_iota(jnp.int32, (layers + 2 * HALO, 1, 1), 0).astype(F32)
    charge = sum(jnp.where(layer == b[line_of_layer, 0], b[None], 0.0) for b in blocks)
    rhs = whole + seam - charge
    mass = 6.0 + charge / 4.0
    inside = (layer >= 0) & (layer < ns * layers)
    inside = inside & ((line < rows) | ((line < rows + 4) & (e < ne - 1)) | ((line >= rows + 4) & (e > 0)))
    inverse = jnp.where(inside, 1.0 / mass, 0.0)
    w0 = inverse * rhs
    w1 = inverse[1:-1] * neighbours(w0)
    w2 = inverse[2:-2] * neighbours(w1)
    n2 = neighbours(w2)[:, :rows]
    w0 = w0[HALO:-HALO, :rows]
    w1 = w1[HALO - 1 : 1 - HALO, :rows]
    w2 = w2[HALO - 2 : 2 - HALO, :rows]
    own_mass = mass[HALO:-HALO, :rows]
    m1, m2 = own_mass * w1, own_mass * w2
    moments = jnp.stack(
        [
            jnp.sum(own_mass * w0 * w0),
            jnp.sum(w0 * m1),
            jnp.sum(w1 * m1),
            jnp.sum(w1 * m2),
            jnp.sum(w2 * m2),
            jnp.sum(w2 * n2),
        ]
    )

    column = s * layers + lax.iota(jnp.int32, layers)

    def chosen(number):
        mask = (column == number)[:, None, None]
        return jnp.stack([jnp.sum(jnp.where(mask, f, 0.0), axis=0) for f in (w0, w1, w2, pot)])

    handed = chosen(blocks[1][line_of_layer, 0].astype(jnp.int32))
    on_layer = chosen(block_layer[0]) + moved(handed, "space", -1)

    row = jnp.pad(moments, (0, depth - moments.shape[0]))[None]
    row = summed(row, "space")
    squared = jnp.square(functions.astype(F32))
    parts = jnp.sum(squared[None] * on_layer[:, None], axis=(2, 3))
    total = summed(jnp.concatenate([parts, row], axis=0), "energy")

    u, z = coefficients([total[4, i] for i in range(6)])
    update = u[0] * w0 + u[1] * w1 + u[2] * w2
    residual = own_mass * (z[0] * w0 + z[1] * w1 + z[2] * w2) + z[3] * n2
    onsite = u[0] * total[0] + u[1] * total[1] + u[2] * total[2] + total[3]
    return (pot + update, residual, onsite[None])


def solution(mesh):
    in_specs = (
        P("energy", "space", None, None),
        P("energy"),
        P("space", None, "energy", None),
        P("space"),
        P("space", "energy", None),
        P("space", "energy", None),
    )
    out_specs = (P("space", "energy", None), P("space", "energy", None), P("space", None))
    return jax.shard_map(shards, mesh=mesh, in_specs=in_specs, out_specs=out_specs, check_vma=False)
```

```python
import jax
import jax.numpy as jnp
from jax import lax
from jax.experimental import pallas as pl
from jax.experimental.pallas import tpu as pltpu
from jax.sharding import PartitionSpec as P

ITERS = 3
HALO = 3
F32 = jnp.float32
BF16 = jnp.bfloat16


def moved(value, axis, by):
    count = lax.axis_size(axis)
    pairs = [(i, i + by) for i in range(count) if 0 <= i + by < count]
    return lax.ppermute(value, axis, pairs)


def along_z(field):
    zero = jnp.zeros_like(field[..., :1])
    up = jnp.concatenate([field[..., 1:], zero], axis=-1)
    down = jnp.concatenate([zero, field[..., :-1]], axis=-1)
    return up + down


def neighbours_in_block(field):
    total = along_z(field)
    for dim in (0, 1):
        width = [(0, 0)] * 3
        width[dim] = (1, 1)
        padded = jnp.pad(field, width)
        count = field.shape[dim]
        total = total + lax.slice_in_dim(padded, 0, count, axis=dim)
        total = total + lax.slice_in_dim(padded, 2, count + 2, axis=dim)
    return total


def unpacked_density(packed):
    half = packed.shape[1]
    packed = packed.astype(BF16).astype(F32)
    row = lax.broadcasted_iota(jnp.int32, (half, half), 0)
    col = lax.broadcasted_iota(jnp.int32, (half, half), 1)
    cross, mixed = packed[:half], packed[half : 2 * half]
    first = jnp.where(row < col, 2.0 * mixed, jnp.where(row == col, mixed, 0.0))
    last = jnp.where(row > col, 2.0 * mixed, 0.0)
    last = last + jnp.where(row == col, packed[2 * half][None], 0.0)
    top = jnp.concatenate([first, 2.0 * cross], axis=1)
    bottom = jnp.concatenate([jnp.zeros_like(last), last], axis=1)
    return jnp.concatenate([top, bottom], axis=0).astype(BF16)


def coefficients(m):
    def inner(a, b, low=0):
        return sum(
            x * y * (m[i + j] - m[i + j + 1] if low else m[i + j])
            for i, x in enumerate(a)
            for j, y in enumerate(b)
        )

    z, d, u, norm = [1.0], [1.0], [], m[0]
    for step in range(ITERS):
        alpha = norm / inner(d, d, 1)
        u = [a + alpha * b for a, b in zip(u + [0.0], d)]
        shifted = [0.0] + d
        z = [a - alpha * (b - c) for a, b, c in zip(z + [0.0], d + [0.0], shifted)]
        if step < ITERS - 1:
            after = inner(z, z)
            d = [a + after / norm * b for a, b in zip(z, d + [0.0])]
            norm = after
    return u, z


def gathered(copies, axis):
    return lax.all_to_all(copies, axis, 0, 0, tiled=True)


def kernel_call(body, *shapes, spaces):
    out = [jax.ShapeDtypeStruct(shape, dtype) for shape, dtype in shapes]
    whole = pl.BlockSpec(memory_space=pltpu.VMEM)
    scalars = pl.BlockSpec(memory_space=pltpu.SMEM)
    return pl.pallas_call(
        body,
        out_shape=out,
        in_specs=[scalars if c == "s" else whole for c in spaces],
        out_specs=[whole] * len(out),
        compiler_params=pltpu.CompilerParams(vmem_limit_bytes=32 * 2**20),
    )


def pack_kernel(weights, green, copies):
    count, size = green.shape[0], green.shape[1]
    half = size // 2
    row = lax.broadcasted_iota(jnp.int32, (half, half), 0)
    col = lax.broadcasted_iota(jnp.int32, (half, half), 1)

    def quarter(i, j):
        rows, cols = slice(i * half, (i + 1) * half), slice(j * half, (j + 1) * half)
        return sum(weights[e] * green[e, rows, cols].astype(F32) for e in range(count))

    low = quarter(1, 1)
    cross = quarter(0, 1).astype(BF16)
    mixed = jnp.where(row <= col, quarter(0, 0), low).astype(BF16)
    diagonal = jnp.sum(jnp.where(row == col, low, 0.0), axis=0, keepdims=True)
    tail = jnp.broadcast_to(diagonal, (16, half)).astype(BF16)
    for target in range(copies.shape[0]):
        copies[target, :half] = cross
        copies[target, half : 2 * half] = mixed
        copies[target, 2 * half :] = tail


def edges_kernel(number, base, pot, charge, above, below, up, down, block):
    layers, rows, depth = pot.shape
    edge = above.shape[1]
    line = lax.broadcasted_iota(jnp.int32, (rows + 2 * edge, depth), 0)
    wide = line.shape[0]

    def joined(own, index):
        return jnp.concatenate([own, above[index], below[index]], axis=0)

    ahead_here = (line == rows) | (line == 0)
    behind_here = (line == rows - 1) | (line == wide - 1)
    for x in range(layers):
        potential = joined(pot[x], layers + x)
        value = joined(base[x], x)
        value = value + jnp.where(ahead_here, pltpu.roll(potential, 1, 0), 0.0)
        value = value + jnp.where(behind_here, pltpu.roll(potential, wide - 1, 0), 0.0)
        if x > layers - 1 - HALO:
            up[x - (layers - HALO)] = value
        if x < HALO:
            down[x] = value
        if x == layers - 1:
            up[HALO] = potential
        if x == 0:
            down[HALO] = potential
    own = joined(charge[...], 2 * layers)
    own = jnp.where(line == rows + HALO, number[0].astype(F32), own)
    up[HALO + 1] = own
    down[HALO + 1] = own
    block[...] = own


def powers_kernel(place, up, down, low, high, lowest, pot, w, mass_out, n2_out, handed, mine, copies):
    layers, rows, depth = pot.shape
    e, s, ne, ns, number = (place[i] for i in range(5))
    wide = up.shape[1]
    edge = (wide - rows) // 2
    line = lax.broadcasted_iota(jnp.int32, (wide, depth), 0)
    cell = lax.broadcasted_iota(jnp.int32, (wide, depth), 1)
    not_first, not_last = cell > 0, cell < depth - 1
    inside = line < rows
    inside = inside | ((line < rows + edge) & (e < ne - 1))
    inside = inside | ((line >= rows + edge) & (e > 0))

    def neighbours(v, x):
        centre = v[x]
        total = pltpu.roll(centre, 1, 0) + pltpu.roll(centre, wide - 1, 0)
        total = total + jnp.where(not_first, pltpu.roll(centre, 1, 1), 0.0)
        total = total + jnp.where(not_last, pltpu.roll(centre, depth - 1, 1), 0.0)
        return total + v[x - 1] + v[x + 1]

    blocks = [lowest[...], low[HALO + 1], up[HALO + 1], high[HALO + 1]]
    ids = [b[rows + HALO : rows + HALO + 1] for b in blocks]
    w0, inverse, mass = {}, {}, {}
    for x in range(-HALO, layers + HALO):
        layer = s * layers + x
        if x < 0:
            value = low[x + HALO]
        elif x < HALO:
            value = down[x]
        elif x < layers:
            value = up[x - (layers - HALO)]
        else:
            value = high[x - layers]
        if x == -1:
            value = value + down[HALO]
        if x == 0:
            value = value + low[HALO]
        if x == layers - 1:
            value = value + high[HALO]
        if x == layers:
            value = value + up[HALO]
        charge = jnp.zeros((wide, depth), F32)
        for b, i in zip(blocks, ids):
            charge = charge + jnp.where(i == layer.astype(F32), b, 0.0)
        mass[x] = 6.0 + charge * 0.25
        valid = inside & (layer >= 0) & (layer < ns * layers)
        inverse[x] = jnp.where(valid, 1.0 / mass[x], 0.0)
        w0[x] = inverse[x] * (value - charge)
    w1 = {x: inverse[x] * neighbours(w0, x) for x in range(1 - HALO, layers + HALO - 1)}
    w2 = {x: inverse[x] * neighbours(w1, x) for x in range(2 - HALO, layers + HALO - 2)}
    sums = [jnp.zeros((rows, depth), F32)] * 6
    on_mine = [jnp.zeros((rows, depth), F32)] * 4
    on_handed = [jnp.zeros((rows, depth), F32)] * 4
    for x in range(layers):
        m, a, b, c = (v[x][:rows] for v in (mass, w0, w1, w2))
        n2 = neighbours(w2, x)[:rows]
        mb, mc = m * b, m * c
        terms = (m * a * a, a * mb, b * mb, b * mc, c * mc, c * n2)
        sums = [t + u for t, u in zip(sums, terms)]
        w[0, x], w[1, x], w[2, x] = a, b, c
        mass_out[x] = m
        n2_out[x] = n2
        layer = s * layers + x
        fields = (a, b, c, pot[x])
        on_mine = [t + jnp.where(number == layer, u, 0.0) for t, u in zip(on_mine, fields)]
        theirs = ids[1] == layer.astype(F32)
        on_handed = [t + jnp.where(theirs, u, 0.0) for t, u in zip(on_handed, fields)]
    for k in range(4):
        mine[k] = on_mine[k]
        handed[k] = on_handed[k]
    lane = lax.broadcasted_iota(jnp.int32, (1, copies.shape[1]), 1)
    row = jnp.zeros(lane.shape, F32)
    for k in range(6):
        row = row + jnp.where(lane == k, jnp.sum(sums[k], keepdims=True), 0.0)
    copies[...] = jnp.broadcast_to(row, copies.shape)


def finish_kernel(parts, w, mass, n2, pot, potential, residual, onsite):
    total = parts[0]
    for i in range(1, parts.shape[0]):
        total = total + parts[i]
    u, z = coefficients([total[4:5, i : i + 1] for i in range(6)])
    for x in range(pot.shape[0]):
        a, b, c = w[0, x], w[1, x], w[2, x]
        potential[x] = pot[x] + (u[0] * a + u[1] * b + u[2] * c)
        residual[x] = mass[x] * (z[0] * a + z[1] * b + z[2] * c) + z[3] * n2[x]
    onsite[...] = u[0] * total[0:1] + u[1] * total[1:2] + u[2] * total[2:3] + total[3:4]


def shards(green, weights, basis, block_layer, pot, dop):
    layers, rows, depth = pot.shape
    e, s = lax.axis_index("energy"), lax.axis_index("space")
    ne, ns = lax.axis_size("energy"), lax.axis_size("space")
    functions = basis[0]
    size = functions.shape[0]
    energies = green.shape[0]
    wide = rows + 8
    block = (layers, rows, depth)
    place = jnp.stack([e, s, ne, ns, block_layer[0]]).astype(jnp.int32)

    packed_shape = (ne, size + 16, size // 2)
    (copies,) = kernel_call(pack_kernel, (packed_shape, BF16), spaces="sv")(
        weights, green.reshape(energies, size, size)
    )
    packed = jnp.sum(gathered(copies, "energy").astype(F32), axis=0)
    density = unpacked_density(packed)
    applied = jnp.einsum("ij,jyz->iyz", density, functions, preferred_element_type=F32)
    charge_block = jnp.sum(functions * applied, axis=0)

    base = dop - 6.0 * pot + neighbours_in_block(pot)
    fields = jnp.concatenate([base, pot, charge_block[None]], axis=0)
    above = moved(fields[:, :4], "energy", -1)
    below = moved(fields[:, -4:], "energy", 1)
    message = ((HALO + 2, wide, depth), F32)
    up, down, own = kernel_call(
        edges_kernel, message, message, ((wide, depth), F32), spaces="svvvvv"
    )(block_layer, base, pot, charge_block, above, below)
    lowest = moved(own, "space", 2)
    low = moved(up, "space", 1)
    high = moved(down, "space", -1)

    field, four = (block, F32), ((4, rows, depth), F32)
    w, mass, n2, handed, mine, copies = kernel_call(
        powers_kernel,
        ((3,) + block, F32),
        field,
        field,
        four,
        four,
        ((ns, 128), F32),
        spaces="svvvvvv",
    )(place, up, down, low, high, lowest, pot)
    row = jnp.sum(gathered(copies, "space"), axis=0)
    on_layer = mine + moved(handed, "space", -1)
    squared = jnp.square(functions.astype(F32))
    parts = jnp.sum(squared[None] * on_layer[:, None], axis=(2, 3))
    row = jnp.pad(row[None], ((0, 3), (0, size - 128)))
    parts = jnp.concatenate([parts, row], axis=0)
    parts = gathered(jnp.broadcast_to(parts[None], (ne,) + parts.shape), "energy")
    potential, residual, onsite = kernel_call(
        finish_kernel, field, field, ((1, size), F32), spaces="vvvvv"
    )(parts, w, mass, n2, pot)
    return (potential, residual, onsite)


def solution(mesh):
    in_specs = (
        P("energy", "space", None, None),
        P("energy"),
        P("space", None, "energy", None),
        P("space"),
        P("space", "energy", None),
        P("space", "energy", None),
    )
    out_specs = (P("space", "energy", None), P("space", "energy", None), P("space", None))
    return jax.shard_map(shards, mesh=mesh, in_specs=in_specs, out_specs=out_specs, check_vma=False)
```

```python
import jax
import jax.numpy as jnp
from jax import lax
from jax.experimental import pallas as pl
from jax.experimental.pallas import tpu as pltpu
from jax.sharding import PartitionSpec as P

ITERS = 3
HALO = 3
F32 = jnp.float32
BF16 = jnp.bfloat16


def moved(value, axis, by):
    count = lax.axis_size(axis)
    pairs = [(i, i + by) for i in range(count) if 0 <= i + by < count]
    return lax.ppermute(value, axis, pairs)


def along_z(field):
    zero = jnp.zeros_like(field[..., :1])
    up = jnp.concatenate([field[..., 1:], zero], axis=-1)
    down = jnp.concatenate([zero, field[..., :-1]], axis=-1)
    return up + down


def neighbours_in_block(field):
    total = along_z(field)
    for dim in (0, 1):
        width = [(0, 0)] * 3
        width[dim] = (1, 1)
        padded = jnp.pad(field, width)
        count = field.shape[dim]
        total = total + lax.slice_in_dim(padded, 0, count, axis=dim)
        total = total + lax.slice_in_dim(padded, 2, count + 2, axis=dim)
    return total


def unpacked_density(packed):
    half = packed.shape[1]
    packed = packed.astype(BF16).astype(F32)
    row = lax.broadcasted_iota(jnp.int32, (half, half), 0)
    col = lax.broadcasted_iota(jnp.int32, (half, half), 1)
    cross, mixed = packed[:half], packed[half : 2 * half]
    first = jnp.where(row < col, 2.0 * mixed, jnp.where(row == col, mixed, 0.0))
    last = jnp.where(row > col, 2.0 * mixed, 0.0)
    last = last + jnp.where(row == col, packed[2 * half][None], 0.0)
    top = jnp.concatenate([first, 2.0 * cross], axis=1)
    bottom = jnp.concatenate([jnp.zeros_like(last), last], axis=1)
    return jnp.concatenate([top, bottom], axis=0).astype(BF16)


def coefficients(m):
    gaps = [a - b for a, b in zip(m, m[1:])]

    def norm_of(a, weights):
        total = 0.0
        for i, x in enumerate(a):
            total = total + x * x * weights[2 * i]
            for j in range(i + 1, len(a)):
                total = total + 2.0 * x * a[j] * weights[i + j]
        return total

    z, d, u, norm = [1.0], [1.0], [], m[0]
    for step in range(ITERS):
        alpha = norm / norm_of(d, gaps)
        u = [a + alpha * b for a, b in zip(u + [0.0], d)]
        shifted = [0.0] + d
        z = [a - alpha * (b - c) for a, b, c in zip(z + [0.0], d + [0.0], shifted)]
        if step < ITERS - 1:
            after = norm_of(z, m)
            ratio = after / norm
            d = [a + ratio * b for a, b in zip(z, d + [0.0])]
            norm = after
    return u, z


def gathered(copies, axis):
    return lax.all_to_all(copies, axis, 0, 0, tiled=True)


def kernel_call(body, *shapes, spaces, scratch=(), cost=None):
    out = [jax.ShapeDtypeStruct(shape, dtype) for shape, dtype in shapes]
    whole = pl.BlockSpec(memory_space=pltpu.VMEM)
    scalars = pl.BlockSpec(memory_space=pltpu.SMEM)
    return pl.pallas_call(
        body,
        out_shape=out,
        in_specs=[scalars if c == "s" else whole for c in spaces],
        out_specs=[whole] * len(out),
        scratch_shapes=scratch,
        cost_estimate=cost,
        compiler_params=pltpu.CompilerParams(vmem_limit_bytes=32 * 2**20),
    )


def pack_kernel(weights, green, copies):
    count, size = green.shape[0], green.shape[1]
    half = size // 2
    row = lax.broadcasted_iota(jnp.int32, (half, half), 0)
    col = lax.broadcasted_iota(jnp.int32, (half, half), 1)

    def quarter(i, j):
        rows, cols = slice(i * half, (i + 1) * half), slice(j * half, (j + 1) * half)
        return sum(
            weights[:, e : e + 1] * green[e, rows, cols].astype(F32) for e in range(count)
        )

    low = quarter(1, 1)
    cross = quarter(0, 1).astype(BF16)
    mixed = jnp.where(row <= col, quarter(0, 0), low).astype(BF16)
    diagonal = jnp.sum(jnp.where(row == col, low, 0.0), axis=0, keepdims=True)
    tail = jnp.broadcast_to(diagonal, (16, half)).astype(BF16)
    for target in range(copies.shape[0]):
        copies[target, :half] = cross
        copies[target, half : 2 * half] = mixed
        copies[target, 2 * half :] = tail


def edges_kernel(number, base, pot, charge, above, below, up, down, block):
    layers, rows, depth = pot.shape
    edge = above.shape[1]
    line = lax.broadcasted_iota(jnp.int32, (rows + 2 * edge, depth), 0)
    wide = line.shape[0]

    def joined(own, index):
        return jnp.concatenate([own, above[index], below[index]], axis=0)

    ahead_here = (line == rows) | (line == 0)
    behind_here = (line == rows - 1) | (line == wide - 1)
    for x in range(layers):
        potential = joined(pot[x], layers + x)
        value = joined(base[x], x)
        value = value + jnp.where(ahead_here, pltpu.roll(potential, 1, 0), 0.0)
        value = value + jnp.where(behind_here, pltpu.roll(potential, wide - 1, 0), 0.0)
        if x > layers - 1 - HALO:
            up[x - (layers - HALO)] = value
        if x < HALO:
            down[x] = value
        if x == layers - 1:
            up[HALO] = potential
        if x == 0:
            down[HALO] = potential
    own = joined(charge[...], 2 * layers)
    own = jnp.where(line == rows + HALO, number[0].astype(F32), own)
    up[HALO + 1] = own
    down[HALO + 1] = own
    block[...] = own


def powers_kernel(place, up, down, low, high, lowest, pot, w, mass_out, n2_out, handed, mine, copies):
    layers, rows, depth = pot.shape
    e, s, ne, ns, number = (place[i] for i in range(5))
    wide = up.shape[1]
    edge = (wide - rows) // 2
    line = lax.broadcasted_iota(jnp.int32, (wide, depth), 0)
    cell = lax.broadcasted_iota(jnp.int32, (wide, depth), 1)
    not_first, not_last = cell > 0, cell < depth - 1
    inside = line < rows
    inside = inside | ((line < rows + edge) & (e < ne - 1))
    inside = inside | ((line >= rows + edge) & (e > 0))

    def neighbours(v, x):
        centre = v[x]
        total = pltpu.roll(centre, 1, 0) + pltpu.roll(centre, wide - 1, 0)
        total = total + jnp.where(not_first, pltpu.roll(centre, 1, 1), 0.0)
        total = total + jnp.where(not_last, pltpu.roll(centre, depth - 1, 1), 0.0)
        return total + v[x - 1] + v[x + 1]

    blocks = [lowest[...], low[HALO + 1], up[HALO + 1], high[HALO + 1]]
    ids = [b[rows + HALO : rows + HALO + 1] for b in blocks]
    w0, inverse, mass = {}, {}, {}
    for x in range(-HALO, layers + HALO):
        layer = s * layers + x
        if x < 0:
            value = low[x + HALO]
        elif x < HALO:
            value = down[x]
        elif x < layers:
            value = up[x - (layers - HALO)]
        else:
            value = high[x - layers]
        if x == -1:
            value = value + down[HALO]
        if x == 0:
            value = value + low[HALO]
        if x == layers - 1:
            value = value + high[HALO]
        if x == layers:
            value = value + up[HALO]
        charge = jnp.zeros((wide, depth), F32)
        for b, i in zip(blocks, ids):
            charge = charge + jnp.where(i == layer.astype(F32), b, 0.0)
        mass[x] = 6.0 + charge * 0.25
        valid = inside & (layer >= 0) & (layer < ns * layers)
        inverse[x] = jnp.where(valid, 1.0 / mass[x], 0.0)
        w0[x] = inverse[x] * (value - charge)
    w1 = {x: inverse[x] * neighbours(w0, x) for x in range(1 - HALO, layers + HALO - 1)}
    w2 = {x: inverse[x] * neighbours(w1, x) for x in range(2 - HALO, layers + HALO - 2)}
    sums = [jnp.zeros((rows, depth), F32)] * 6
    on_mine = [jnp.zeros((rows, depth), F32)] * 4
    on_handed = [jnp.zeros((rows, depth), F32)] * 4
    for x in range(layers):
        m, a, b, c = (v[x][:rows] for v in (mass, w0, w1, w2))
        n2 = neighbours(w2, x)[:rows]
        mb, mc = m * b, m * c
        terms = (m * a * a, a * mb, b * mb, b * mc, c * mc, c * n2)
        sums = [t + u for t, u in zip(sums, terms)]
        w[0, x], w[1, x], w[2, x] = a, b, c
        mass_out[x] = m
        n2_out[x] = n2
        layer = s * layers + x
        fields = (a, b, c, pot[x])
        on_mine = [t + jnp.where(number == layer, u, 0.0) for t, u in zip(on_mine, fields)]
        theirs = ids[1] == layer.astype(F32)
        on_handed = [t + jnp.where(theirs, u, 0.0) for t, u in zip(on_handed, fields)]
    for k in range(4):
        mine[k] = on_mine[k]
        handed[k] = on_handed[k]
    lane = lax.broadcasted_iota(jnp.int32, (1, copies.shape[1]), 1)
    row = jnp.zeros(lane.shape, F32)
    for k in range(6):
        row = row + jnp.where(lane == k, jnp.sum(sums[k], keepdims=True), 0.0)
    copies[...] = jnp.broadcast_to(row, copies.shape)


def onsite_kernel(basis, mine, theirs, out, sums):
    size, rows, depth = basis.shape
    chunk = 64
    field = (mine[...] + theirs[...]).reshape(4 * rows, depth)
    pieces = []
    for _ in range(3):
        piece = field.astype(BF16)
        pieces.append(piece)
        field = field - piece.astype(F32)
    pieces.append(jnp.zeros_like(piece))
    values = jnp.concatenate(pieces, axis=0)
    lanes = values.shape[0]
    contract = (((1,), (1,)), ((), ()))
    here = lax.broadcasted_iota(jnp.int32, (rows, lanes), 0)
    there = lax.broadcasted_iota(jnp.int32, (rows, lanes), 1)
    same = (there % rows == here).astype(F32)
    for start in range(0, size, chunk):
        part = basis[start : start + chunk].astype(F32)
        squared = (part * part).reshape(chunk * rows, depth)
        high = squared.astype(BF16)
        low = (squared - high.astype(F32)).astype(BF16)
        product = lax.dot_general(high, values, contract, preferred_element_type=F32)
        product = product + lax.dot_general(low, values, contract, preferred_element_type=F32)
        product = product.reshape(chunk, rows, lanes) * same[None]
        sums[start : start + chunk] = jnp.sum(product, axis=1)
    out_row = lax.broadcasted_iota(jnp.int32, (8, lanes), 0)
    out_lane = lax.broadcasted_iota(jnp.int32, (8, lanes), 1)
    pick = (out_lane % (4 * rows)) // rows == out_row
    pick = (pick & (out_lane < 12 * rows)).astype(F32)
    result = lax.dot_general(
        pick, sums[...], contract, precision=lax.Precision.HIGHEST, preferred_element_type=F32
    )
    out[...] = result


def finish_kernel(parts, w, mass, n2, pot, potential, residual, onsite):
    total = parts[0]
    for i in range(1, parts.shape[0]):
        total = total + parts[i]
    u, z = coefficients([total[4:5, i : i + 1] for i in range(6)])
    for x in range(pot.shape[0]):
        a, b, c = w[0, x], w[1, x], w[2, x]
        potential[x] = pot[x] + (u[0] * a + u[1] * b + u[2] * c)
        residual[x] = mass[x] * (z[0] * a + z[1] * b + z[2] * c) + z[3] * n2[x]
    onsite[...] = u[0] * total[0:1] + u[1] * total[1:2] + u[2] * total[2:3] + total[3:4]


def shards(green, weights, basis, block_layer, pot, dop):
    layers, rows, depth = pot.shape
    e, s = lax.axis_index("energy"), lax.axis_index("space")
    ne, ns = lax.axis_size("energy"), lax.axis_size("space")
    functions = basis[0]
    size = functions.shape[0]
    energies = green.shape[0]
    wide = rows + 8
    block = (layers, rows, depth)
    place = jnp.stack([e, s, ne, ns, block_layer[0]]).astype(jnp.int32)

    packed_shape = (ne, size + 16, size // 2)
    (copies,) = kernel_call(pack_kernel, (packed_shape, BF16), spaces="vv")(
        weights[None], green.reshape(energies, size, size)
    )
    packed = jnp.sum(gathered(copies, "energy").astype(F32), axis=0)
    density = unpacked_density(packed)
    applied = jnp.einsum("ij,jyz->iyz", density, functions, preferred_element_type=F32)
    charge_block = jnp.sum(functions * applied, axis=0)

    base = dop - 6.0 * pot + neighbours_in_block(pot)
    fields = jnp.concatenate([base, pot, charge_block[None]], axis=0)
    above = moved(fields[:, :4], "energy", -1)
    below = moved(fields[:, -4:], "energy", 1)
    message = ((HALO + 2, wide, depth), F32)
    up, down, own = kernel_call(
        edges_kernel, message, message, ((wide, depth), F32), spaces="svvvvv"
    )(block_layer, base, pot, charge_block, above, below)
    lowest = moved(own, "space", 2)
    low = moved(up, "space", 1)
    high = moved(down, "space", -1)

    field, four = (block, F32), ((4, rows, depth), F32)
    w, mass, n2, handed, mine, copies = kernel_call(
        powers_kernel,
        ((3,) + block, F32),
        field,
        field,
        four,
        four,
        ((ns, 128), F32),
        spaces="svvvvvv",
    )(place, up, down, low, high, lowest, pot)
    row = jnp.sum(gathered(copies, "space"), axis=0)
    theirs = moved(handed, "space", -1)
    (parts,) = kernel_call(
        onsite_kernel,
        ((8, size), F32),
        spaces="vvv",
        scratch=[pltpu.VMEM((size, 16 * rows), F32)],
        cost=pl.CostEstimate(
            flops=2 * 256 * size * rows * depth, bytes_accessed=2 * size * rows * depth, transcendentals=0
        ),
    )(functions, mine, theirs)
    row = jnp.pad(row[None], ((4, 3), (0, size - 128)))
    parts = parts + row
    parts = gathered(jnp.broadcast_to(parts[None], (ne,) + parts.shape), "energy")
    potential, residual, onsite = kernel_call(
        finish_kernel, field, field, ((1, size), F32), spaces="vvvvv"
    )(parts, w, mass, n2, pot)
    return (potential, residual, onsite)


def solution(mesh):
    in_specs = (
        P("energy", "space", None, None),
        P("energy"),
        P("space", None, "energy", None),
        P("space"),
        P("space", "energy", None),
        P("space", "energy", None),
    )
    out_specs = (P("space", "energy", None), P("space", "energy", None), P("space", None))
    return jax.shard_map(shards, mesh=mesh, in_specs=in_specs, out_specs=out_specs, check_vma=False)
```

```python
import jax
import jax.numpy as jnp
from jax import lax
from jax.experimental import pallas as pl
from jax.experimental.pallas import tpu as pltpu
from jax.sharding import PartitionSpec as P

ITERS = 3
HALO = 3
F32 = jnp.float32
BF16 = jnp.bfloat16


def moved(value, axis, by):
    count = lax.axis_size(axis)
    pairs = [(i, i + by) for i in range(count) if 0 <= i + by < count]
    return lax.ppermute(value, axis, pairs)


def along_z(field):
    zero = jnp.zeros_like(field[..., :1])
    up = jnp.concatenate([field[..., 1:], zero], axis=-1)
    down = jnp.concatenate([zero, field[..., :-1]], axis=-1)
    return up + down


def neighbours_in_block(field):
    total = along_z(field)
    for dim in (0, 1):
        width = [(0, 0)] * 3
        width[dim] = (1, 1)
        padded = jnp.pad(field, width)
        count = field.shape[dim]
        total = total + lax.slice_in_dim(padded, 0, count, axis=dim)
        total = total + lax.slice_in_dim(padded, 2, count + 2, axis=dim)
    return total


def unpacked_density(packed):
    half = packed.shape[1]
    packed = packed.astype(BF16).astype(F32)
    row = lax.broadcasted_iota(jnp.int32, (half, half), 0)
    col = lax.broadcasted_iota(jnp.int32, (half, half), 1)
    cross, mixed = packed[:half], packed[half : 2 * half]
    first = jnp.where(row < col, 2.0 * mixed, jnp.where(row == col, mixed, 0.0))
    last = jnp.where(row > col, 2.0 * mixed, 0.0)
    last = last + jnp.where(row == col, packed[2 * half][None], 0.0)
    top = jnp.concatenate([first, 2.0 * cross], axis=1)
    bottom = jnp.concatenate([jnp.zeros_like(last), last], axis=1)
    return jnp.concatenate([top, bottom], axis=0).astype(BF16)


def coefficients(m):
    gaps = [a - b for a, b in zip(m, m[1:])]

    def norm_of(a, weights):
        total = 0.0
        for i, x in enumerate(a):
            total = total + x * x * weights[2 * i]
            for j in range(i + 1, len(a)):
                total = total + 2.0 * x * a[j] * weights[i + j]
        return total

    z, d, u, norm = [1.0], [1.0], [], m[0]
    for step in range(ITERS):
        alpha = norm / norm_of(d, gaps)
        u = [a + alpha * b for a, b in zip(u + [0.0], d)]
        shifted = [0.0] + d
        z = [a - alpha * (b - c) for a, b, c in zip(z + [0.0], d + [0.0], shifted)]
        if step < ITERS - 1:
            after = norm_of(z, m)
            ratio = after / norm
            d = [a + ratio * b for a, b in zip(z, d + [0.0])]
            norm = after
    return u, z


def gathered(copies, axis):
    return lax.all_to_all(copies, axis, 0, 0, tiled=True)


def kernel_call(body, *shapes, spaces, scratch=(), cost=None, room=32):
    out = [jax.ShapeDtypeStruct(shape, dtype) for shape, dtype in shapes]
    whole = pl.BlockSpec(memory_space=pltpu.VMEM)
    scalars = pl.BlockSpec(memory_space=pltpu.SMEM)
    return pl.pallas_call(
        body,
        out_shape=out,
        in_specs=[scalars if c == "s" else whole for c in spaces],
        out_specs=[whole] * len(out),
        scratch_shapes=scratch,
        cost_estimate=cost,
        compiler_params=pltpu.CompilerParams(vmem_limit_bytes=room * 2**20),
    )


def pack_kernel(weights, green, copies):
    count, size = green.shape[0], green.shape[1]
    half = size // 2
    row = lax.broadcasted_iota(jnp.int32, (half, half), 0)
    col = lax.broadcasted_iota(jnp.int32, (half, half), 1)

    def quarter(i, j):
        rows, cols = slice(i * half, (i + 1) * half), slice(j * half, (j + 1) * half)
        return sum(
            weights[:, e : e + 1] * green[e, rows, cols].astype(F32) for e in range(count)
        )

    low = quarter(1, 1)
    cross = quarter(0, 1).astype(BF16)
    mixed = jnp.where(row <= col, quarter(0, 0), low).astype(BF16)
    diagonal = jnp.sum(jnp.where(row == col, low, 0.0), axis=0, keepdims=True)
    tail = jnp.broadcast_to(diagonal, (16, half)).astype(BF16)
    for target in range(copies.shape[0]):
        copies[target, :half] = cross
        copies[target, half : 2 * half] = mixed
        copies[target, 2 * half :] = tail


def edges_kernel(place, base, pot, charge, pair, pair_charge, outer, up, down, block):
    layers, rows, depth = pot.shape
    edge = outer.shape[1]
    even = place[0] % 2 == 0
    number = place[4]
    line = lax.broadcasted_iota(jnp.int32, (rows + 2 * edge, depth), 0)
    wide = line.shape[0]

    def joined(own, index):
        inner = pair[index] if index < 2 * layers else pair_charge[...]
        above = jnp.where(even, inner, outer[index])
        below = jnp.where(even, outer[index], inner)
        return jnp.concatenate([own, above, below], axis=0)

    ahead_here = (line == rows) | (line == 0)
    behind_here = (line == rows - 1) | (line == wide - 1)
    for x in range(layers):
        potential = joined(pot[x], layers + x)
        value = joined(base[x], x)
        value = value + jnp.where(ahead_here, pltpu.roll(potential, 1, 0), 0.0)
        value = value + jnp.where(behind_here, pltpu.roll(potential, wide - 1, 0), 0.0)
        if x > layers - 1 - HALO:
            up[x - (layers - HALO)] = value
        if x < HALO:
            down[x] = value
        if x == layers - 1:
            up[HALO] = potential
        if x == 0:
            down[HALO] = potential
    own = joined(charge[...], 2 * layers)
    own = jnp.where(line == rows + HALO, number.astype(F32), own)
    up[HALO + 1] = own
    down[HALO + 1] = own
    block[...] = own


def powers_kernel(place, up, down, low, high, lowest, pot, w, mass_out, n2_out, handed, mine, copies):
    layers, rows, depth = pot.shape
    e, s, ne, ns, number = (place[i] for i in range(5))
    wide = up.shape[1]
    edge = (wide - rows) // 2
    line = lax.broadcasted_iota(jnp.int32, (wide, depth), 0)
    cell = lax.broadcasted_iota(jnp.int32, (wide, depth), 1)
    not_first, not_last = cell > 0, cell < depth - 1
    inside = line < rows
    inside = inside | ((line < rows + edge) & (e < ne - 1))
    inside = inside | ((line >= rows + edge) & (e > 0))

    def neighbours(v, x):
        centre = v[x]
        total = pltpu.roll(centre, 1, 0) + pltpu.roll(centre, wide - 1, 0)
        total = total + jnp.where(not_first, pltpu.roll(centre, 1, 1), 0.0)
        total = total + jnp.where(not_last, pltpu.roll(centre, depth - 1, 1), 0.0)
        return total + v[x - 1] + v[x + 1]

    blocks = [lowest[...], low[HALO + 1], up[HALO + 1], high[HALO + 1]]
    ids = [b[rows + HALO : rows + HALO + 1] for b in blocks]
    w0, inverse, mass = {}, {}, {}
    for x in range(-HALO, layers + HALO):
        layer = s * layers + x
        if x < 0:
            value = low[x + HALO]
        elif x < HALO:
            value = down[x]
        elif x < layers:
            value = up[x - (layers - HALO)]
        else:
            value = high[x - layers]
        if x == -1:
            value = value + down[HALO]
        if x == 0:
            value = value + low[HALO]
        if x == layers - 1:
            value = value + high[HALO]
        if x == layers:
            value = value + up[HALO]
        charge = jnp.zeros((wide, depth), F32)
        for b, i in zip(blocks, ids):
            charge = charge + jnp.where(i == layer.astype(F32), b, 0.0)
        mass[x] = 6.0 + charge * 0.25
        valid = inside & (layer >= 0) & (layer < ns * layers)
        inverse[x] = jnp.where(valid, 1.0 / mass[x], 0.0)
        w0[x] = inverse[x] * (value - charge)
    w1 = {x: inverse[x] * neighbours(w0, x) for x in range(1 - HALO, layers + HALO - 1)}
    w2 = {x: inverse[x] * neighbours(w1, x) for x in range(2 - HALO, layers + HALO - 2)}
    sums = [jnp.zeros((rows, depth), F32)] * 6
    on_mine = [jnp.zeros((rows, depth), F32)] * 4
    on_handed = [jnp.zeros((rows, depth), F32)] * 4
    for x in range(layers):
        m, a, b, c = (v[x][:rows] for v in (mass, w0, w1, w2))
        n2 = neighbours(w2, x)[:rows]
        mb, mc = m * b, m * c
        terms = (m * a * a, a * mb, b * mb, b * mc, c * mc, c * n2)
        sums = [t + u for t, u in zip(sums, terms)]
        w[0, x], w[1, x], w[2, x] = a, b, c
        mass_out[x] = m
        n2_out[x] = n2
        layer = s * layers + x
        fields = (a, b, c, pot[x])
        on_mine = [t + jnp.where(number == layer, u, 0.0) for t, u in zip(on_mine, fields)]
        theirs = ids[1] == layer.astype(F32)
        on_handed = [t + jnp.where(theirs, u, 0.0) for t, u in zip(on_handed, fields)]
    for k in range(4):
        mine[k] = on_mine[k]
        handed[k] = on_handed[k]
    lane = lax.broadcasted_iota(jnp.int32, (1, copies.shape[1]), 1)
    row = jnp.zeros(lane.shape, F32)
    for k in range(6):
        row = row + jnp.where(lane == k, jnp.sum(sums[k], keepdims=True), 0.0)
    copies[...] = jnp.broadcast_to(row, copies.shape)


def onsite_kernel(basis, mine, theirs, out, sums):
    _, size, rows, depth = basis.shape
    chunk = 64
    field = (mine[...] + theirs[...]).reshape(4 * rows, depth)
    pieces = []
    for _ in range(3):
        piece = field.astype(BF16)
        pieces.append(piece)
        field = field - piece.astype(F32)
    pieces.append(jnp.zeros_like(piece))
    values = jnp.concatenate(pieces, axis=0)
    lanes = values.shape[0]
    contract = (((1,), (1,)), ((), ()))
    here = lax.broadcasted_iota(jnp.int32, (rows, lanes), 0)
    there = lax.broadcasted_iota(jnp.int32, (rows, lanes), 1)
    same = (there % rows == here).astype(F32)
    for start in range(0, size, chunk):
        part = basis[0, start : start + chunk].astype(F32)
        squared = (part * part).reshape(chunk * rows, depth)
        high = squared.astype(BF16)
        low = (squared - high.astype(F32)).astype(BF16)
        product = lax.dot_general(high, values, contract, preferred_element_type=F32)
        product = product + lax.dot_general(low, values, contract, preferred_element_type=F32)
        product = product.reshape(chunk, rows, lanes) * same[None]
        sums[start : start + chunk] = jnp.sum(product, axis=1)
    out_row = lax.broadcasted_iota(jnp.int32, (8, lanes), 0)
    out_lane = lax.broadcasted_iota(jnp.int32, (8, lanes), 1)
    pick = (out_lane % (4 * rows)) // rows == out_row
    pick = (pick & (out_lane < 12 * rows)).astype(F32)
    result = lax.dot_general(
        pick, sums[...], contract, precision=lax.Precision.HIGHEST, preferred_element_type=F32
    )
    out[...] = result


def finish_kernel(parts, w, mass, n2, pot, potential, residual, onsite):
    total = parts[0]
    for i in range(1, parts.shape[0]):
        total = total + parts[i]
    u, z = coefficients([total[4:5, i : i + 1] for i in range(6)])
    for x in range(pot.shape[0]):
        a, b, c = w[0, x], w[1, x], w[2, x]
        potential[x] = pot[x] + (u[0] * a + u[1] * b + u[2] * c)
        residual[x] = mass[x] * (z[0] * a + z[1] * b + z[2] * c) + z[3] * n2[x]
    onsite[...] = u[0] * total[0:1] + u[1] * total[1:2] + u[2] * total[2:3] + total[3:4]


def shards(green, weights, basis, block_layer, pot, dop):
    layers, rows, depth = pot.shape
    e, s = lax.axis_index("energy"), lax.axis_index("space")
    ne, ns = lax.axis_size("energy"), lax.axis_size("space")
    functions = basis[0]
    size = functions.shape[0]
    energies = green.shape[0]
    wide = rows + 8
    block = (layers, rows, depth)
    place = jnp.stack([e, s, ne, ns, block_layer[0]]).astype(jnp.int32)

    packed_shape = (ne, size + 16, size // 2)
    (copies,) = kernel_call(pack_kernel, (packed_shape, BF16), spaces="vv", room=60)(
        weights[None], green.reshape(energies, size, size)
    )
    even = e % 2 == 0
    pairs = [(i, i ^ 1) for i in range(ne)]
    across = [(i, i + 1) for i in range(1, ne - 1, 2)]
    across = across + [(target, source) for source, target in across]

    def near_pair(value):
        return jnp.where(even, value[:, -4:], value[:, :4])

    late_basis, late_pot, late_dop, copies = lax.optimization_barrier((basis, pot, dop, copies))
    base = late_dop - 6.0 * late_pot + neighbours_in_block(late_pot)
    fields = jnp.concatenate([base, late_pot], axis=0)
    pair_basis = lax.ppermute(near_pair(late_basis[0]), "energy", pairs)
    pair_fields = lax.ppermute(near_pair(fields), "energy", pairs)

    packed = jnp.sum(gathered(copies, "energy").astype(F32), axis=0)
    density = unpacked_density(packed)

    def charge_of(values):
        applied = jnp.einsum("ij,jyz->iyz", density, values, preferred_element_type=F32)
        return jnp.sum(values * applied, axis=0)

    charge_block = charge_of(functions)
    pair_charge = charge_of(pair_basis)
    fields = jnp.concatenate([fields, charge_block[None]], axis=0)
    outer = jnp.where(even, fields[:, :4], fields[:, -4:])
    outer = lax.ppermute(outer, "energy", across)
    message = ((HALO + 2, wide, depth), F32)
    up, down, own = kernel_call(
        edges_kernel, message, message, ((wide, depth), F32), spaces="svvvvvv"
    )(place, base, pot, charge_block, pair_fields, pair_charge, outer)
    lowest = moved(own, "space", 2)
    low = moved(up, "space", 1)
    high = moved(down, "space", -1)

    field, four = (block, F32), ((4, rows, depth), F32)
    w, mass, n2, handed, mine, copies = kernel_call(
        powers_kernel,
        ((3,) + block, F32),
        field,
        field,
        four,
        four,
        ((ns, 128), F32),
        spaces="svvvvvv",
    )(place, up, down, low, high, lowest, pot)
    row = jnp.sum(gathered(copies, "space"), axis=0)
    theirs = moved(handed, "space", -1)
    (parts,) = kernel_call(
        onsite_kernel,
        ((8, size), F32),
        spaces="vvv",
        scratch=[pltpu.VMEM((size, 16 * rows), F32)],
        cost=pl.CostEstimate(
            flops=2 * 256 * size * rows * depth, bytes_accessed=2 * size * rows * depth, transcendentals=0
        ),
    )(basis, mine, theirs)
    row = jnp.pad(row[None], ((4, 3), (0, size - 128)))
    parts = parts + row
    parts = gathered(jnp.broadcast_to(parts[None], (ne,) + parts.shape), "energy")
    potential, residual, onsite = kernel_call(
        finish_kernel, field, field, ((1, size), F32), spaces="vvvvv"
    )(parts, w, mass, n2, pot)
    return (potential, residual, onsite)


def solution(mesh):
    in_specs = (
        P("energy", "space", None, None),
        P("energy"),
        P("space", None, "energy", None),
        P("space"),
        P("space", "energy", None),
        P("space", "energy", None),
    )
    out_specs = (P("space", "energy", None), P("space", "energy", None), P("space", None))
    return jax.shard_map(shards, mesh=mesh, in_specs=in_specs, out_specs=out_specs, check_vma=False)
```

```python
import jax
import jax.numpy as jnp
from jax import lax
from jax.experimental import pallas as pl
from jax.experimental.pallas import tpu as pltpu
from jax.sharding import PartitionSpec as P

ITERS = 3
HALO = 3
F32 = jnp.float32
BF16 = jnp.bfloat16


def moved(value, axis, by):
    count = lax.axis_size(axis)
    pairs = [(i, i + by) for i in range(count) if 0 <= i + by < count]
    return lax.ppermute(value, axis, pairs)


def along_z(field):
    zero = jnp.zeros_like(field[..., :1])
    up = jnp.concatenate([field[..., 1:], zero], axis=-1)
    down = jnp.concatenate([zero, field[..., :-1]], axis=-1)
    return up + down


def neighbours_in_block(field):
    total = along_z(field)
    for dim in (0, 1):
        width = [(0, 0)] * 3
        width[dim] = (1, 1)
        padded = jnp.pad(field, width)
        count = field.shape[dim]
        total = total + lax.slice_in_dim(padded, 0, count, axis=dim)
        total = total + lax.slice_in_dim(padded, 2, count + 2, axis=dim)
    return total


def unpacked_density(packed):
    half = packed.shape[1]
    packed = packed.astype(BF16).astype(F32)
    row = lax.broadcasted_iota(jnp.int32, (half, half), 0)
    col = lax.broadcasted_iota(jnp.int32, (half, half), 1)
    cross, mixed = packed[:half], packed[half : 2 * half]
    first = jnp.where(row < col, 2.0 * mixed, jnp.where(row == col, mixed, 0.0))
    last = jnp.where(row > col, 2.0 * mixed, 0.0)
    last = last + jnp.where(row == col, packed[2 * half][None], 0.0)
    top = jnp.concatenate([first, 2.0 * cross], axis=1)
    bottom = jnp.concatenate([jnp.zeros_like(last), last], axis=1)
    return jnp.concatenate([top, bottom], axis=0).astype(BF16)


def coefficients(m):
    gaps = [a - b for a, b in zip(m, m[1:])]

    def norm_of(a, weights):
        total = 0.0
        for i, x in enumerate(a):
            total = total + x * x * weights[2 * i]
            for j in range(i + 1, len(a)):
                total = total + 2.0 * x * a[j] * weights[i + j]
        return total

    z, d, u, norm = [1.0], [1.0], [], m[0]
    for step in range(ITERS):
        alpha = norm / norm_of(d, gaps)
        u = [a + alpha * b for a, b in zip(u + [0.0], d)]
        shifted = [0.0] + d
        z = [a - alpha * (b - c) for a, b, c in zip(z + [0.0], d + [0.0], shifted)]
        if step < ITERS - 1:
            after = norm_of(z, m)
            ratio = after / norm
            d = [a + ratio * b for a, b in zip(z, d + [0.0])]
            norm = after
    return u, z


def gathered(copies, axis):
    return lax.all_to_all(copies, axis, 0, 0, tiled=True)


def kernel_call(body, *shapes, spaces, scratch=(), cost=None, room=32):
    out = [jax.ShapeDtypeStruct(shape, dtype) for shape, dtype in shapes]
    whole = pl.BlockSpec(memory_space=pltpu.VMEM)
    scalars = pl.BlockSpec(memory_space=pltpu.SMEM)
    return pl.pallas_call(
        body,
        out_shape=out,
        in_specs=[scalars if c == "s" else whole for c in spaces],
        out_specs=[whole] * len(out),
        scratch_shapes=scratch,
        cost_estimate=cost,
        compiler_params=pltpu.CompilerParams(vmem_limit_bytes=room * 2**20),
    )


def pack_kernel(weights, green, copies):
    count, size = green.shape[0], green.shape[1]
    half = size // 2
    row = lax.broadcasted_iota(jnp.int32, (half, half), 0)
    col = lax.broadcasted_iota(jnp.int32, (half, half), 1)

    def quarter(i, j):
        rows, cols = slice(i * half, (i + 1) * half), slice(j * half, (j + 1) * half)
        return sum(
            weights[:, e : e + 1] * green[e, rows, cols].astype(F32) for e in range(count)
        )

    low = quarter(1, 1)
    cross = quarter(0, 1).astype(BF16)
    mixed = jnp.where(row <= col, quarter(0, 0), low).astype(BF16)
    diagonal = jnp.sum(jnp.where(row == col, low, 0.0), axis=0, keepdims=True)
    tail = jnp.broadcast_to(diagonal, (16, half)).astype(BF16)
    for target in range(copies.shape[0]):
        copies[target, :half] = cross
        copies[target, half : 2 * half] = mixed
        copies[target, 2 * half :] = tail


def edges_kernel(place, base, pot, charge, pair, pair_charge, outer, up, down, block):
    layers, rows, depth = pot.shape
    edge = outer.shape[1]
    even = jnp.broadcast_to(place[0:1], (edge, depth)) > 0.5
    number = place[1:2]
    line = lax.broadcasted_iota(jnp.int32, (rows + 2 * edge, depth), 0)
    wide = line.shape[0]

    def joined(own, index):
        inner = pair[index] if index < 2 * layers else pair_charge[...]
        above = jnp.where(even, inner, outer[index])
        below = jnp.where(even, outer[index], inner)
        return jnp.concatenate([own, above, below], axis=0)

    ahead_here = (line == rows) | (line == 0)
    behind_here = (line == rows - 1) | (line == wide - 1)
    for x in range(layers):
        potential = joined(pot[x], layers + x)
        value = joined(base[x], x)
        value = value + jnp.where(ahead_here, pltpu.roll(potential, 1, 0), 0.0)
        value = value + jnp.where(behind_here, pltpu.roll(potential, wide - 1, 0), 0.0)
        if x > layers - 1 - HALO:
            up[x - (layers - HALO)] = value
        if x < HALO:
            down[x] = value
        if x == layers - 1:
            up[HALO] = potential
        if x == 0:
            down[HALO] = potential
    own = joined(charge[...], 2 * layers)
    own = jnp.where(line == rows + HALO, number, own)
    up[HALO + 1] = own
    down[HALO + 1] = own
    block[...] = own


def arrived_kernel(place, up, lowest, low, charge):
    rows = up.shape[1] - 8
    first = place[2:3]
    blocks = [lowest[...], low[HALO + 1], up[HALO + 1]]
    ids = [b[rows + HALO : rows + HALO + 1] for b in blocks]
    for x in range(charge.shape[0]):
        layer = first + float(x - HALO)
        total = jnp.zeros(lowest.shape, F32)
        for b, i in zip(blocks, ids):
            total = total + jnp.where(i == layer, b, 0.0)
        charge[x] = total


def powers_kernel(place, up, down, part, low, high, pot, w, mass_out, n2_out, handed, mine, copies):
    layers, rows, depth = pot.shape
    number, first = place[1:2], place[2:3]
    after_all = float(layers * copies.shape[0])
    wide = up.shape[1]
    edge = (wide - rows) // 2
    line = lax.broadcasted_iota(jnp.int32, (wide, depth), 0)
    cell = lax.broadcasted_iota(jnp.int32, (wide, depth), 1)
    not_first, not_last = cell > 0, cell < depth - 1
    inside = line < rows
    inside = inside | ((line < rows + edge) & (place[3:4] > 0.5))
    inside = inside | ((line >= rows + edge) & (place[4:5] > 0.5))

    def neighbours(v, x):
        centre = v[x]
        total = pltpu.roll(centre, 1, 0) + pltpu.roll(centre, wide - 1, 0)
        total = total + jnp.where(not_first, pltpu.roll(centre, 1, 1), 0.0)
        total = total + jnp.where(not_last, pltpu.roll(centre, depth - 1, 1), 0.0)
        return total + v[x - 1] + v[x + 1]

    last = high[HALO + 1]
    low_id, last_id = (b[HALO + 1, rows + HALO : rows + HALO + 1] for b in (low, high))
    w0, inverse, mass = {}, {}, {}
    for x in range(-HALO, layers + HALO):
        layer = first + float(x)
        if x < 0:
            value = low[x + HALO]
        elif x < HALO:
            value = down[x]
        elif x < layers:
            value = up[x - (layers - HALO)]
        else:
            value = high[x - layers]
        if x == -1:
            value = value + down[HALO]
        if x == 0:
            value = value + low[HALO]
        if x == layers - 1:
            value = value + high[HALO]
        if x == layers:
            value = value + up[HALO]
        charge = part[x + HALO] + jnp.where(last_id == layer, last, 0.0)
        mass[x] = 6.0 + charge * 0.25
        valid = inside & (layer > -0.5) & (layer < after_all - 0.5)
        inverse[x] = jnp.where(valid, 1.0 / mass[x], 0.0)
        w0[x] = inverse[x] * (value - charge)
    w1 = {x: inverse[x] * neighbours(w0, x) for x in range(1 - HALO, layers + HALO - 1)}
    w2 = {x: inverse[x] * neighbours(w1, x) for x in range(2 - HALO, layers + HALO - 2)}
    sums = [jnp.zeros((rows, depth), F32)] * 6
    on_mine = [jnp.zeros((rows, depth), F32)] * 4
    on_handed = [jnp.zeros((rows, depth), F32)] * 4
    for x in range(layers):
        m, a, b, c = (v[x][:rows] for v in (mass, w0, w1, w2))
        n2 = neighbours(w2, x)[:rows]
        mb, mc = m * b, m * c
        terms = (m * a * a, a * mb, b * mb, b * mc, c * mc, c * n2)
        sums = [t + u for t, u in zip(sums, terms)]
        w[0, x], w[1, x], w[2, x] = a, b, c
        mass_out[x] = m
        n2_out[x] = n2
        layer = first + float(x)
        fields = (a, b, c, pot[x])
        on_mine = [t + jnp.where(number == layer, u, 0.0) for t, u in zip(on_mine, fields)]
        theirs = low_id == layer
        on_handed = [t + jnp.where(theirs, u, 0.0) for t, u in zip(on_handed, fields)]
    for k in range(4):
        mine[k] = on_mine[k]
        handed[k] = on_handed[k]
    lane = lax.broadcasted_iota(jnp.int32, (1, copies.shape[1]), 1)
    row = jnp.zeros(lane.shape, F32)
    for k in range(6):
        row = row + jnp.where(lane == k, jnp.sum(sums[k], keepdims=True), 0.0)
    copies[...] = jnp.broadcast_to(row, copies.shape)


def onsite_kernel(basis, mine, theirs, out, sums):
    _, size, rows, depth = basis.shape
    chunk = 64
    field = (mine[...] + theirs[...]).reshape(4 * rows, depth)
    pieces = []
    for _ in range(3):
        piece = field.astype(BF16)
        pieces.append(piece)
        field = field - piece.astype(F32)
    pieces.append(jnp.zeros_like(piece))
    values = jnp.concatenate(pieces, axis=0)
    lanes = values.shape[0]
    contract = (((1,), (1,)), ((), ()))
    here = lax.broadcasted_iota(jnp.int32, (rows, lanes), 0)
    there = lax.broadcasted_iota(jnp.int32, (rows, lanes), 1)
    same = (there % rows == here).astype(F32)
    for start in range(0, size, chunk):
        part = basis[0, start : start + chunk].astype(F32)
        squared = (part * part).reshape(chunk * rows, depth)
        high = squared.astype(BF16)
        low = (squared - high.astype(F32)).astype(BF16)
        product = lax.dot_general(high, values, contract, preferred_element_type=F32)
        product = product + lax.dot_general(low, values, contract, preferred_element_type=F32)
        product = product.reshape(chunk, rows, lanes) * same[None]
        sums[start : start + chunk] = jnp.sum(product, axis=1)
    out_row = lax.broadcasted_iota(jnp.int32, (8, lanes), 0)
    out_lane = lax.broadcasted_iota(jnp.int32, (8, lanes), 1)
    pick = (out_lane % (4 * rows)) // rows == out_row
    pick = (pick & (out_lane < 12 * rows)).astype(F32)
    result = lax.dot_general(
        pick, sums[...], contract, precision=lax.Precision.HIGHEST, preferred_element_type=F32
    )
    out[...] = result


def finish_kernel(parts, w, mass, n2, pot, potential, residual, onsite):
    total = parts[0]
    for i in range(1, parts.shape[0]):
        total = total + parts[i]
    u, z = coefficients([total[4:5, i : i + 1] for i in range(6)])
    for x in range(pot.shape[0]):
        a, b, c = w[0, x], w[1, x], w[2, x]
        potential[x] = pot[x] + (u[0] * a + u[1] * b + u[2] * c)
        residual[x] = mass[x] * (z[0] * a + z[1] * b + z[2] * c) + z[3] * n2[x]
    onsite[...] = u[0] * total[0:1] + u[1] * total[1:2] + u[2] * total[2:3] + total[3:4]


def shards(green, weights, basis, block_layer, pot, dop):
    layers, rows, depth = pot.shape
    e, s = lax.axis_index("energy"), lax.axis_index("space")
    ne, ns = lax.axis_size("energy"), lax.axis_size("space")
    functions = basis[0]
    size = functions.shape[0]
    energies = green.shape[0]
    wide = rows + 8
    block = (layers, rows, depth)
    facts = [e % 2 == 0, block_layer[0], s * layers, e < ne - 1, e > 0, 0, 0, 0]
    place = jnp.broadcast_to(jnp.stack([jnp.asarray(f, F32) for f in facts])[:, None], (8, depth))

    packed_shape = (ne, size + 16, size // 2)
    (copies,) = kernel_call(pack_kernel, (packed_shape, BF16), spaces="vv", room=60)(
        weights[None], green.reshape(energies, size, size)
    )
    even = e % 2 == 0
    pairs = [(i, i ^ 1) for i in range(ne)]
    across = [(i, i + 1) for i in range(1, ne - 1, 2)]
    across = across + [(target, source) for source, target in across]

    def near_pair(value):
        return jnp.where(even, value[:, -4:], value[:, :4])

    late_basis, late_pot, late_dop, copies = lax.optimization_barrier((basis, pot, dop, copies))
    base = late_dop - 6.0 * late_pot + neighbours_in_block(late_pot)
    fields = jnp.concatenate([base, late_pot], axis=0)
    pair_basis = lax.ppermute(near_pair(late_basis[0]), "energy", pairs)
    pair_fields = lax.ppermute(near_pair(fields), "energy", pairs)

    packed = jnp.sum(gathered(copies, "energy").astype(F32), axis=0)
    density = unpacked_density(packed)

    def charge_of(values):
        applied = jnp.einsum("ij,jyz->iyz", density, values, preferred_element_type=F32)
        return jnp.sum(values * applied, axis=0)

    charge_block = charge_of(functions)
    pair_charge = charge_of(pair_basis)
    fields = jnp.concatenate([fields, charge_block[None]], axis=0)
    outer = jnp.where(even, fields[:, :4], fields[:, -4:])
    outer = lax.ppermute(outer, "energy", across)
    message = ((HALO + 2, wide, depth), F32)
    up, down, own = kernel_call(
        edges_kernel, message, message, ((wide, depth), F32), spaces="vvvvvvv"
    )(place, base, pot, charge_block, pair_fields, pair_charge, outer)
    lowest = moved(own, "space", 2)
    low = moved(up, "space", 1)
    high = moved(down, "space", -1)

    (part,) = kernel_call(
        arrived_kernel,
        ((layers + 2 * HALO, wide, depth), F32),
        spaces="vvvv",
        cost=pl.CostEstimate(flops=8 * 10**9, bytes_accessed=10**6, transcendentals=0),
    )(place, up, lowest, low)
    field, four = (block, F32), ((4, rows, depth), F32)
    w, mass, n2, handed, mine, copies = kernel_call(
        powers_kernel,
        ((3,) + block, F32),
        field,
        field,
        four,
        four,
        ((ns, 128), F32),
        spaces="vvvvvvv",
    )(place, up, down, part, low, high, pot)
    row = jnp.sum(gathered(copies, "space"), axis=0)
    theirs = moved(handed, "space", -1)
    (parts,) = kernel_call(
        onsite_kernel,
        ((8, size), F32),
        spaces="vvv",
        scratch=[pltpu.VMEM((size, 16 * rows), F32)],
        cost=pl.CostEstimate(
            flops=2 * 256 * size * rows * depth, bytes_accessed=2 * size * rows * depth, transcendentals=0
        ),
    )(basis, mine, theirs)
    row = jnp.pad(row[None], ((4, 3), (0, size - 128)))
    parts = parts + row
    parts = gathered(jnp.broadcast_to(parts[None], (ne,) + parts.shape), "energy")
    potential, residual, onsite = kernel_call(
        finish_kernel, field, field, ((1, size), F32), spaces="vvvvv"
    )(parts, w, mass, n2, pot)
    return (potential, residual, onsite)


def solution(mesh):
    in_specs = (
        P("energy", "space", None, None),
        P("energy"),
        P("space", None, "energy", None),
        P("space"),
        P("space", "energy", None),
        P("space", "energy", None),
    )
    out_specs = (P("space", "energy", None), P("space", "energy", None), P("space", None))
    return jax.shard_map(shards, mesh=mesh, in_specs=in_specs, out_specs=out_specs, check_vma=False)
```

```python
import jax
import jax.numpy as jnp
from jax import lax
from jax.experimental import pallas as pl
from jax.experimental.pallas import tpu as pltpu
from jax.sharding import PartitionSpec as P

ITERS = 3
HALO = 3
F32 = jnp.float32
BF16 = jnp.bfloat16


def moved(value, axis, by):
    count = lax.axis_size(axis)
    pairs = [(i, i + by) for i in range(count) if 0 <= i + by < count]
    return lax.ppermute(value, axis, pairs)


def along_z(field):
    zero = jnp.zeros_like(field[..., :1])
    up = jnp.concatenate([field[..., 1:], zero], axis=-1)
    down = jnp.concatenate([zero, field[..., :-1]], axis=-1)
    return up + down


def neighbours_in_block(field):
    total = along_z(field)
    for dim in (0, 1):
        width = [(0, 0)] * 3
        width[dim] = (1, 1)
        padded = jnp.pad(field, width)
        count = field.shape[dim]
        total = total + lax.slice_in_dim(padded, 0, count, axis=dim)
        total = total + lax.slice_in_dim(padded, 2, count + 2, axis=dim)
    return total


def coefficients(m):
    gaps = [a - b for a, b in zip(m, m[1:])]

    def norm_of(a, weights):
        total = 0.0
        for i, x in enumerate(a):
            total = total + x * x * weights[2 * i]
            for j in range(i + 1, len(a)):
                total = total + 2.0 * x * a[j] * weights[i + j]
        return total

    z, d, u, norm = [1.0], [1.0], [], m[0]
    for step in range(ITERS):
        alpha = norm / norm_of(d, gaps)
        u = [a + alpha * b for a, b in zip(u + [0.0], d)]
        shifted = [0.0] + d
        z = [a - alpha * (b - c) for a, b, c in zip(z + [0.0], d + [0.0], shifted)]
        if step < ITERS - 1:
            after = norm_of(z, m)
            ratio = after / norm
            d = [a + ratio * b for a, b in zip(z, d + [0.0])]
            norm = after
    return u, z


def gathered(copies, axis):
    return lax.all_to_all(copies, axis, 0, 0, tiled=True)


def kernel_call(body, *shapes, spaces, scratch=(), cost=None, room=32):
    out = [jax.ShapeDtypeStruct(shape, dtype) for shape, dtype in shapes]
    whole = pl.BlockSpec(memory_space=pltpu.VMEM)
    scalars = pl.BlockSpec(memory_space=pltpu.SMEM)
    return pl.pallas_call(
        body,
        out_shape=out,
        in_specs=[scalars if c == "s" else whole for c in spaces],
        out_specs=[whole] * len(out),
        scratch_shapes=scratch,
        cost_estimate=cost,
        compiler_params=pltpu.CompilerParams(vmem_limit_bytes=room * 2**20),
    )


def pack_kernel(weights, green, copies):
    count, size = green.shape[0], green.shape[1]
    half = size // 2
    row = lax.broadcasted_iota(jnp.int32, (half, half), 0)
    col = lax.broadcasted_iota(jnp.int32, (half, half), 1)

    def quarter(i, j):
        rows, cols = slice(i * half, (i + 1) * half), slice(j * half, (j + 1) * half)
        return sum(
            weights[:, e : e + 1] * green[e, rows, cols].astype(F32) for e in range(count)
        )

    low = quarter(1, 1)
    cross = quarter(0, 1).astype(BF16)
    mixed = jnp.where(row <= col, quarter(0, 0), low).astype(BF16)
    diagonal = jnp.sum(jnp.where(row == col, low, 0.0), axis=0, keepdims=True)
    tail = jnp.broadcast_to(diagonal, (16, half)).astype(BF16)
    for target in range(copies.shape[0]):
        copies[target, :half] = cross
        copies[target, half : 2 * half] = mixed
        copies[target, 2 * half :] = tail


def unpack_kernel(copies, density):
    half = density.shape[0] // 2

    def total(rows):
        parts = copies[0, rows].astype(F32)
        for i in range(1, copies.shape[0]):
            parts = parts + copies[i, rows].astype(F32)
        return parts.astype(BF16).astype(F32)

    row = lax.broadcasted_iota(jnp.int32, (half, half), 0)
    col = lax.broadcasted_iota(jnp.int32, (half, half), 1)
    cross = total(slice(0, half))
    mixed = total(slice(half, 2 * half))
    diagonal = total(slice(2 * half, 2 * half + 16))[:1]
    first = jnp.where(row < col, 2.0 * mixed, jnp.where(row == col, mixed, 0.0))
    last = jnp.where(row > col, 2.0 * mixed, jnp.where(row == col, diagonal, 0.0))
    density[:half, :half] = first.astype(BF16)
    density[:half, half:] = (2.0 * cross).astype(BF16)
    density[half:, :half] = jnp.zeros((half, half), BF16)
    density[half:, half:] = last.astype(BF16)


def in_three(value):
    pieces = []
    for _ in range(3):
        piece = lax.reduce_precision(value, 8, 7)
        pieces.append(piece.astype(BF16))
        value = value - piece
    return pieces


def edges_kernel(
    place, base, pot, charge, pair, pair_charge, outer, outer_charge, up, down, block
):
    layers, rows, depth = pot.shape
    even = jnp.broadcast_to(place[0:1], (HALO, depth)) > 0.5
    number = place[1:2]
    wide = rows + 8
    line = lax.broadcasted_iota(jnp.int32, (wide, depth), 0)
    gap = jnp.zeros((wide - rows - 2 * HALO, depth), F32)

    def joined(own, inner, far):
        above = jnp.where(even, inner, far)
        below = jnp.where(even, far, inner)
        return jnp.concatenate([own, above, gap, below], axis=0)

    ahead_here = (line == rows) | (line == 0)
    behind_here = (line == rows - 1) | (line == wide - 1)
    for x in range(layers):
        potential = joined(pot[x], pair[layers + x], outer[layers + x])
        value = joined(base[x], pair[x], outer[x])
        value = value + jnp.where(ahead_here, pltpu.roll(potential, 1, 0), 0.0)
        value = value + jnp.where(behind_here, pltpu.roll(potential, wide - 1, 0), 0.0)
        if x > layers - 1 - HALO:
            up[x - (layers - HALO)] = value
        if x < HALO:
            down[x] = value
        if x == layers - 1:
            up[HALO] = potential
        if x == 0:
            down[HALO] = potential
    own = joined(charge[...], pair_charge[...], outer_charge[...])
    own = jnp.where(line == rows + HALO, number, own)
    up[HALO + 1] = own
    down[HALO + 1] = own
    block[...] = own


def arrived_kernel(place, up, lowest, low, charge):
    rows = up.shape[1] - 8
    first = place[2:3]
    blocks = [lowest[...], low[HALO + 1], up[HALO + 1]]
    ids = [b[rows + HALO : rows + HALO + 1] for b in blocks]
    for x in range(charge.shape[0]):
        layer = first + float(x - HALO)
        total = jnp.zeros(lowest.shape, F32)
        for b, i in zip(blocks, ids):
            total = total + jnp.where(i == layer, b, 0.0)
        charge[x] = total


def powers_kernel(place, up, down, part, low, high, pot, w, mass_out, n2_out, handed, mine, copies):
    layers, rows, depth = pot.shape
    number, first = place[1:2], place[2:3]
    after_all = float(layers * copies.shape[0])
    wide = up.shape[1]
    edge = (wide - rows) // 2
    line = lax.broadcasted_iota(jnp.int32, (wide, depth), 0)
    cell = lax.broadcasted_iota(jnp.int32, (wide, depth), 1)
    not_first, not_last = cell > 0, cell < depth - 1
    inside = line < rows
    inside = inside | ((line < rows + edge) & (place[3:4] > 0.5))
    inside = inside | ((line >= rows + edge) & (place[4:5] > 0.5))

    def neighbours(v, x):
        centre = v[x]
        total = pltpu.roll(centre, 1, 0) + pltpu.roll(centre, wide - 1, 0)
        total = total + jnp.where(not_first, pltpu.roll(centre, 1, 1), 0.0)
        total = total + jnp.where(not_last, pltpu.roll(centre, depth - 1, 1), 0.0)
        return total + v[x - 1] + v[x + 1]

    last = high[HALO + 1]
    low_id, last_id = (b[HALO + 1, rows + HALO : rows + HALO + 1] for b in (low, high))
    w0, inverse, mass = {}, {}, {}
    for x in range(-HALO, layers + HALO):
        layer = first + float(x)
        if x < 0:
            value = low[x + HALO]
        elif x < HALO:
            value = down[x]
        elif x < layers:
            value = up[x - (layers - HALO)]
        else:
            value = high[x - layers]
        if x == -1:
            value = value + down[HALO]
        if x == 0:
            value = value + low[HALO]
        if x == layers - 1:
            value = value + high[HALO]
        if x == layers:
            value = value + up[HALO]
        charge = part[x + HALO] + jnp.where(last_id == layer, last, 0.0)
        mass[x] = 6.0 + charge * 0.25
        valid = inside & (layer > -0.5) & (layer < after_all - 0.5)
        inverse[x] = jnp.where(valid, 1.0 / mass[x], 0.0)
        w0[x] = inverse[x] * (value - charge)
    w1 = {x: inverse[x] * neighbours(w0, x) for x in range(1 - HALO, layers + HALO - 1)}
    w2 = {x: inverse[x] * neighbours(w1, x) for x in range(2 - HALO, layers + HALO - 2)}
    sums = [jnp.zeros((rows, depth), F32)] * 6
    on_mine = [jnp.zeros((rows, depth), F32)] * 4
    on_handed = [jnp.zeros((rows, depth), F32)] * 4
    for x in range(layers):
        m, a, b, c = (v[x][:rows] for v in (mass, w0, w1, w2))
        n2 = neighbours(w2, x)[:rows]
        mb, mc = m * b, m * c
        terms = (m * a * a, a * mb, b * mb, b * mc, c * mc, c * n2)
        sums = [t + u for t, u in zip(sums, terms)]
        w[0, x], w[1, x], w[2, x] = a, b, c
        mass_out[x] = m
        n2_out[x] = n2
        layer = first + float(x)
        fields = (a, b, c, pot[x])
        on_mine = [t + jnp.where(number == layer, u, 0.0) for t, u in zip(on_mine, fields)]
        theirs = low_id == layer
        on_handed = [t + jnp.where(theirs, u, 0.0) for t, u in zip(on_handed, fields)]
    for k in range(4):
        mine[k] = on_mine[k]
        handed[k] = on_handed[k]
    lane = lax.broadcasted_iota(jnp.int32, (1, copies.shape[1]), 1)
    row = jnp.zeros(lane.shape, F32)
    for k in range(6):
        row = row + jnp.where(lane == k, jnp.sum(sums[k], keepdims=True), 0.0)
    copies[...] = jnp.broadcast_to(row, copies.shape)


def onsite_kernel(basis, mine, theirs, out, sums):
    _, size, rows, depth = basis.shape
    chunk = 64
    field = (mine[...] + theirs[...]).reshape(4 * rows, depth)
    pieces = []
    for _ in range(3):
        piece = field.astype(BF16)
        pieces.append(piece)
        field = field - piece.astype(F32)
    pieces.append(jnp.zeros_like(piece))
    values = jnp.concatenate(pieces, axis=0)
    lanes = values.shape[0]
    contract = (((1,), (1,)), ((), ()))
    here = lax.broadcasted_iota(jnp.int32, (rows, lanes), 0)
    there = lax.broadcasted_iota(jnp.int32, (rows, lanes), 1)
    same = (there % rows == here).astype(F32)
    for start in range(0, size, chunk):
        part = basis[0, start : start + chunk].astype(F32)
        squared = (part * part).reshape(chunk * rows, depth)
        high = squared.astype(BF16)
        low = (squared - high.astype(F32)).astype(BF16)
        product = lax.dot_general(high, values, contract, preferred_element_type=F32)
        product = product + lax.dot_general(low, values, contract, preferred_element_type=F32)
        product = product.reshape(chunk, rows, lanes) * same[None]
        sums[start : start + chunk] = jnp.sum(product, axis=1)
    out_row = lax.broadcasted_iota(jnp.int32, (8, lanes), 0)
    out_lane = lax.broadcasted_iota(jnp.int32, (8, lanes), 1)
    pick = (out_lane % (4 * rows)) // rows == out_row
    pick = (pick & (out_lane < 12 * rows)).astype(F32)
    result = lax.dot_general(
        pick, sums[...], contract, precision=lax.Precision.HIGHEST, preferred_element_type=F32
    )
    out[...] = result


def finish_kernel(parts, w, mass, n2, pot, potential, residual, onsite):
    total = parts[0]
    for i in range(1, parts.shape[0]):
        total = total + parts[i]
    u, z = coefficients([total[4:5, i : i + 1] for i in range(6)])
    for x in range(pot.shape[0]):
        a, b, c = w[0, x], w[1, x], w[2, x]
        potential[x] = pot[x] + (u[0] * a + u[1] * b + u[2] * c)
        residual[x] = mass[x] * (z[0] * a + z[1] * b + z[2] * c) + z[3] * n2[x]
    onsite[...] = u[0] * total[0:1] + u[1] * total[1:2] + u[2] * total[2:3] + total[3:4]


def shards(green, weights, basis, block_layer, pot, dop):
    layers, rows, depth = pot.shape
    e, s = lax.axis_index("energy"), lax.axis_index("space")
    ne, ns = lax.axis_size("energy"), lax.axis_size("space")
    functions = basis[0]
    size = functions.shape[0]
    energies = green.shape[0]
    wide = rows + 8
    block = (layers, rows, depth)
    facts = [e % 2 == 0, block_layer[0], s * layers, e < ne - 1, e > 0, 0, 0, 0]
    place = jnp.broadcast_to(jnp.stack([jnp.asarray(f, F32) for f in facts])[:, None], (8, depth))

    packed_shape = (ne, size + 16, size // 2)
    (copies,) = kernel_call(pack_kernel, (packed_shape, BF16), spaces="vv", room=60)(
        weights[None], green.reshape(energies, size, size)
    )
    even = e % 2 == 0
    pairs = [(i, i ^ 1) for i in range(ne)]
    across = [(i, i + 1) for i in range(1, ne - 1, 2)]
    across = across + [(target, source) for source, target in across]

    late_basis, late_pot, late_dop, copies = lax.optimization_barrier((basis, pot, dop, copies))
    base = late_dop - 6.0 * late_pot + neighbours_in_block(late_pot)
    fields = jnp.concatenate([base, late_pot], axis=0)
    lines = jnp.concatenate([late_basis[0], *in_three(fields)], axis=0)
    lines = jnp.transpose(lines, (1, 0, 2))
    front, back = lines[:HALO], lines[-HALO:]
    pair = lax.ppermute(jnp.where(even, back, front), "energy", pairs)
    outer = lax.ppermute(jnp.where(even, front, back), "energy", across)

    (density,) = kernel_call(
        unpack_kernel,
        ((size, size), BF16),
        spaces="v",
        cost=pl.CostEstimate(flops=10**10, bytes_accessed=10**6, transcendentals=0),
    )(gathered(copies, "energy"))
    pair, pair_density = lax.optimization_barrier((pair, density))
    applied = jnp.einsum("ij,jyz->iyz", density, functions, preferred_element_type=F32)
    charge_block = jnp.sum(functions * applied, axis=0)

    def from_lines(received, density):
        values = received[:, :size]
        applied = jnp.einsum("ij,yjz->yiz", density, values, preferred_element_type=F32)
        pieces = jnp.split(received[:, size:].astype(F32), 3, axis=1)
        around = jnp.transpose(pieces[0] + pieces[1] + pieces[2], (1, 0, 2))
        return around, jnp.sum(values * applied, axis=1)

    pair_fields, pair_charge = from_lines(pair, pair_density)
    outer, outer_density, charge_block, pair_charge = lax.optimization_barrier(
        (outer, density, charge_block, pair_charge)
    )
    outer_fields, outer_charge = from_lines(outer, outer_density)
    message = ((HALO + 2, wide, depth), F32)
    up, down, own = kernel_call(
        edges_kernel, message, message, ((wide, depth), F32), spaces="vvvvvvvv"
    )(
        place,
        base,
        pot,
        charge_block,
        pair_fields,
        pair_charge,
        outer_fields,
        outer_charge,
    )
    lowest = moved(own, "space", 2)
    low = moved(up, "space", 1)
    high = moved(down, "space", -1)

    (part,) = kernel_call(
        arrived_kernel,
        ((layers + 2 * HALO, wide, depth), F32),
        spaces="vvvv",
        cost=pl.CostEstimate(flops=8 * 10**9, bytes_accessed=10**6, transcendentals=0),
    )(place, up, lowest, low)
    field, four = (block, F32), ((4, rows, depth), F32)
    w, mass, n2, handed, mine, copies = kernel_call(
        powers_kernel,
        ((3,) + block, F32),
        field,
        field,
        four,
        four,
        ((ns, 128), F32),
        spaces="vvvvvvv",
    )(place, up, down, part, low, high, pot)
    row = jnp.sum(gathered(copies, "space"), axis=0)
    theirs = moved(handed, "space", -1)
    (parts,) = kernel_call(
        onsite_kernel,
        ((8, size), F32),
        spaces="vvv",
        scratch=[pltpu.VMEM((size, 16 * rows), F32)],
        cost=pl.CostEstimate(
            flops=2 * 256 * size * rows * depth, bytes_accessed=2 * size * rows * depth, transcendentals=0
        ),
    )(basis, mine, theirs)
    row = jnp.pad(row[None], ((4, 3), (0, size - 128)))
    parts = parts + row
    parts = gathered(jnp.broadcast_to(parts[None], (ne,) + parts.shape), "energy")
    potential, residual, onsite = kernel_call(
        finish_kernel, field, field, ((1, size), F32), spaces="vvvvv"
    )(parts, w, mass, n2, pot)
    return (potential, residual, onsite)


def solution(mesh):
    in_specs = (
        P("energy", "space", None, None),
        P("energy"),
        P("space", None, "energy", None),
        P("space"),
        P("space", "energy", None),
        P("space", "energy", None),
    )
    out_specs = (P("space", "energy", None), P("space", "energy", None), P("space", None))
    return jax.shard_map(shards, mesh=mesh, in_specs=in_specs, out_specs=out_specs, check_vma=False)
```

```python
import jax
import jax.numpy as jnp
from jax import lax
from jax.experimental import pallas as pl
from jax.experimental.pallas import tpu as pltpu
from jax.sharding import PartitionSpec as P

ITERS = 3
HALO = 3
F32 = jnp.float32
BF16 = jnp.bfloat16


def moved(value, axis, by):
    count = lax.axis_size(axis)
    pairs = [(i, i + by) for i in range(count) if 0 <= i + by < count]
    return lax.ppermute(value, axis, pairs)


def along_z(field):
    zero = jnp.zeros_like(field[..., :1])
    up = jnp.concatenate([field[..., 1:], zero], axis=-1)
    down = jnp.concatenate([zero, field[..., :-1]], axis=-1)
    return up + down


def neighbours_in_block(field):
    total = along_z(field)
    for dim in (0, 1):
        width = [(0, 0)] * 3
        width[dim] = (1, 1)
        padded = jnp.pad(field, width)
        count = field.shape[dim]
        total = total + lax.slice_in_dim(padded, 0, count, axis=dim)
        total = total + lax.slice_in_dim(padded, 2, count + 2, axis=dim)
    return total


def coefficients(m):
    gaps = [a - b for a, b in zip(m, m[1:])]

    def norm_of(a, weights):
        total = 0.0
        for i, x in enumerate(a):
            total = total + x * x * weights[2 * i]
            for j in range(i + 1, len(a)):
                total = total + 2.0 * x * a[j] * weights[i + j]
        return total

    z, d, u, norm = [1.0], [1.0], [], m[0]
    for step in range(ITERS):
        alpha = norm / norm_of(d, gaps)
        u = [a + alpha * b for a, b in zip(u + [0.0], d)]
        shifted = [0.0] + d
        z = [a - alpha * (b - c) for a, b, c in zip(z + [0.0], d + [0.0], shifted)]
        if step < ITERS - 1:
            after = norm_of(z, m)
            ratio = after / norm
            d = [a + ratio * b for a, b in zip(z, d + [0.0])]
            norm = after
    return u, z


def gathered(copies, axis):
    return lax.all_to_all(copies, axis, 0, 0, tiled=True)


def kernel_call(body, *shapes, spaces, scratch=(), cost=None, room=32):
    out = [jax.ShapeDtypeStruct(shape, dtype) for shape, dtype in shapes]
    whole = pl.BlockSpec(memory_space=pltpu.VMEM)
    scalars = pl.BlockSpec(memory_space=pltpu.SMEM)
    return pl.pallas_call(
        body,
        out_shape=out,
        in_specs=[scalars if c == "s" else whole for c in spaces],
        out_specs=[whole] * len(out),
        scratch_shapes=scratch,
        cost_estimate=cost,
        compiler_params=pltpu.CompilerParams(vmem_limit_bytes=room * 2**20),
    )


def pack_kernel(weights, green, copies):
    count, size = green.shape[0], green.shape[1]
    half = size // 2
    row = lax.broadcasted_iota(jnp.int32, (half, half), 0)
    col = lax.broadcasted_iota(jnp.int32, (half, half), 1)

    def quarter(i, j):
        rows, cols = slice(i * half, (i + 1) * half), slice(j * half, (j + 1) * half)
        return sum(
            weights[:, e : e + 1] * green[e, rows, cols].astype(F32) for e in range(count)
        )

    low = quarter(1, 1)
    cross = quarter(0, 1).astype(BF16)
    mixed = jnp.where(row <= col, quarter(0, 0), low).astype(BF16)
    diagonal = jnp.sum(jnp.where(row == col, low, 0.0), axis=0, keepdims=True)
    tail = jnp.broadcast_to(diagonal, (16, half)).astype(BF16)
    for target in range(copies.shape[0]):
        copies[target, :half] = cross
        copies[target, half : 2 * half] = mixed
        copies[target, 2 * half :] = tail


def unpack_kernel(copies, density):
    half = density.shape[0] // 2

    def total(rows):
        parts = copies[0, rows].astype(F32)
        for i in range(1, copies.shape[0]):
            parts = parts + copies[i, rows].astype(F32)
        return parts.astype(BF16).astype(F32)

    row = lax.broadcasted_iota(jnp.int32, (half, half), 0)
    col = lax.broadcasted_iota(jnp.int32, (half, half), 1)
    cross = total(slice(0, half))
    mixed = total(slice(half, 2 * half))
    diagonal = total(slice(2 * half, 2 * half + 16))[:1]
    first = jnp.where(row < col, 2.0 * mixed, jnp.where(row == col, mixed, 0.0))
    last = jnp.where(row > col, 2.0 * mixed, jnp.where(row == col, diagonal, 0.0))
    density[:half, :half] = first.astype(BF16)
    density[:half, half:] = (2.0 * cross).astype(BF16)
    density[half:, :half] = jnp.zeros((half, half), BF16)
    density[half:, half:] = last.astype(BF16)


def in_three(value):
    pieces = []
    for _ in range(3):
        piece = lax.reduce_precision(value, 8, 7)
        pieces.append(piece.astype(BF16))
        value = value - piece
    return pieces


def edges_kernel(
    place, base, pot, charge, pair, pair_charge, outer, outer_charge, up, down, block
):
    layers, rows, depth = pot.shape
    even = jnp.broadcast_to(place[0:1], (HALO, depth)) > 0.5
    number = place[1:2]
    wide = rows + 8
    line = lax.broadcasted_iota(jnp.int32, (wide, depth), 0)
    gap = jnp.zeros((wide - rows - 2 * HALO, depth), F32)

    def joined(own, inner, far):
        above = jnp.where(even, inner, far)
        below = jnp.where(even, far, inner)
        return jnp.concatenate([own, above, gap, below], axis=0)

    ahead_here = (line == rows) | (line == 0)
    behind_here = (line == rows - 1) | (line == wide - 1)
    for x in range(layers):
        potential = joined(pot[x], pair[layers + x], outer[layers + x])
        value = joined(base[x], pair[x], outer[x])
        value = value + jnp.where(ahead_here, pltpu.roll(potential, 1, 0), 0.0)
        value = value + jnp.where(behind_here, pltpu.roll(potential, wide - 1, 0), 0.0)
        if x > layers - 1 - HALO:
            up[x - (layers - HALO)] = value
        if x < HALO:
            down[x] = value
        if x == layers - 1:
            up[HALO] = potential
        if x == 0:
            down[HALO] = potential
    own = joined(charge[...], pair_charge[...], outer_charge[...])
    own = jnp.where(line == rows + HALO, number, own)
    up[HALO + 1] = own
    down[HALO + 1] = own
    block[...] = own


def arrived_kernel(place, up, lowest, low, charge):
    rows = up.shape[1] - 8
    first = place[2:3]
    blocks = [lowest[...], low[HALO + 1], up[HALO + 1]]
    ids = [b[rows + HALO : rows + HALO + 1] for b in blocks]
    for x in range(charge.shape[0]):
        layer = first + float(x - HALO)
        total = jnp.zeros(lowest.shape, F32)
        for b, i in zip(blocks, ids):
            total = total + jnp.where(i == layer, b, 0.0)
        charge[x] = total


def powers_kernel(place, up, down, part, low, high, pot, w, mass_out, n2_out, handed, mine, copies):
    layers, rows, depth = pot.shape
    number, first = place[1:2], place[2:3]
    after_all = float(layers * copies.shape[0])
    wide = up.shape[1]
    edge = (wide - rows) // 2
    line = lax.broadcasted_iota(jnp.int32, (wide, depth), 0)
    cell = lax.broadcasted_iota(jnp.int32, (wide, depth), 1)
    not_first, not_last = cell > 0, cell < depth - 1
    inside = line < rows
    inside = inside | ((line < rows + edge) & (place[3:4] > 0.5))
    inside = inside | ((line >= rows + edge) & (place[4:5] > 0.5))

    def neighbours(v, x):
        centre = v[x]
        total = pltpu.roll(centre, 1, 0) + pltpu.roll(centre, wide - 1, 0)
        total = total + jnp.where(not_first, pltpu.roll(centre, 1, 1), 0.0)
        total = total + jnp.where(not_last, pltpu.roll(centre, depth - 1, 1), 0.0)
        return total + v[x - 1] + v[x + 1]

    last = high[HALO + 1]
    low_id, last_id = (b[HALO + 1, rows + HALO : rows + HALO + 1] for b in (low, high))
    w0, inverse, mass = {}, {}, {}
    for x in range(-HALO, layers + HALO):
        layer = first + float(x)
        if x < 0:
            value = low[x + HALO]
        elif x < HALO:
            value = down[x]
        elif x < layers:
            value = up[x - (layers - HALO)]
        else:
            value = high[x - layers]
        if x == -1:
            value = value + down[HALO]
        if x == 0:
            value = value + low[HALO]
        if x == layers - 1:
            value = value + high[HALO]
        if x == layers:
            value = value + up[HALO]
        charge = part[x + HALO] + jnp.where(last_id == layer, last, 0.0)
        mass[x] = 6.0 + charge * 0.25
        valid = inside & (layer > -0.5) & (layer < after_all - 0.5)
        inverse[x] = jnp.where(valid, 1.0 / mass[x], 0.0)
        w0[x] = inverse[x] * (value - charge)
    w1 = {x: inverse[x] * neighbours(w0, x) for x in range(1 - HALO, layers + HALO - 1)}
    w2 = {x: inverse[x] * neighbours(w1, x) for x in range(2 - HALO, layers + HALO - 2)}
    sums = [jnp.zeros((rows, depth), F32)] * 6
    on_mine = [jnp.zeros((rows, depth), F32)] * 4
    on_handed = [jnp.zeros((rows, depth), F32)] * 4
    for x in range(layers):
        m, a, b, c = (v[x][:rows] for v in (mass, w0, w1, w2))
        n2 = neighbours(w2, x)[:rows]
        mb, mc = m * b, m * c
        terms = (m * a * a, a * mb, b * mb, b * mc, c * mc, c * n2)
        sums = [t + u for t, u in zip(sums, terms)]
        w[0, x], w[1, x], w[2, x] = a, b, c
        mass_out[x] = m
        n2_out[x] = n2
        layer = first + float(x)
        fields = (a, b, c, pot[x])
        on_mine = [t + jnp.where(number == layer, u, 0.0) for t, u in zip(on_mine, fields)]
        theirs = low_id == layer
        on_handed = [t + jnp.where(theirs, u, 0.0) for t, u in zip(on_handed, fields)]
    for k in range(4):
        mine[k] = on_mine[k]
        handed[k] = on_handed[k]
    lane = lax.broadcasted_iota(jnp.int32, (1, copies.shape[1]), 1)
    row = jnp.zeros(lane.shape, F32)
    for k in range(6):
        row = row + jnp.where(lane == k, jnp.sum(sums[k], keepdims=True), 0.0)
    copies[...] = jnp.broadcast_to(row, copies.shape)


def onsite_kernel(basis, mine, theirs, out, sums):
    _, size, rows, depth = basis.shape
    chunk = 64
    field = (mine[...] + theirs[...]).reshape(4 * rows, depth)
    pieces = []
    for _ in range(3):
        piece = field.astype(BF16)
        pieces.append(piece)
        field = field - piece.astype(F32)
    pieces.append(jnp.zeros_like(piece))
    values = jnp.concatenate(pieces, axis=0)
    lanes = values.shape[0]
    contract = (((1,), (1,)), ((), ()))
    here = lax.broadcasted_iota(jnp.int32, (rows, lanes), 0)
    there = lax.broadcasted_iota(jnp.int32, (rows, lanes), 1)
    same = (there % rows == here).astype(F32)
    for start in range(0, size, chunk):
        part = basis[0, start : start + chunk].astype(F32)
        squared = (part * part).reshape(chunk * rows, depth)
        high = squared.astype(BF16)
        low = (squared - high.astype(F32)).astype(BF16)
        product = lax.dot_general(high, values, contract, preferred_element_type=F32)
        product = product + lax.dot_general(low, values, contract, preferred_element_type=F32)
        product = product.reshape(chunk, rows, lanes) * same[None]
        sums[start : start + chunk] = jnp.sum(product, axis=1)
    out_row = lax.broadcasted_iota(jnp.int32, (8, lanes), 0)
    out_lane = lax.broadcasted_iota(jnp.int32, (8, lanes), 1)
    pick = (out_lane % (4 * rows)) // rows == out_row
    pick = (pick & (out_lane < 12 * rows)).astype(F32)
    result = lax.dot_general(
        pick, sums[...], contract, precision=lax.Precision.HIGHEST, preferred_element_type=F32
    )
    out[...] = result


def finish_kernel(parts, w, mass, n2, pot, potential, residual, onsite):
    total = parts[0]
    for i in range(1, parts.shape[0]):
        total = total + parts[i]
    u, z = coefficients([total[4:5, i : i + 1] for i in range(6)])
    for x in range(pot.shape[0]):
        a, b, c = w[0, x], w[1, x], w[2, x]
        potential[x] = pot[x] + (u[0] * a + u[1] * b + u[2] * c)
        residual[x] = mass[x] * (z[0] * a + z[1] * b + z[2] * c) + z[3] * n2[x]
    onsite[...] = u[0] * total[0:1] + u[1] * total[1:2] + u[2] * total[2:3] + total[3:4]


def shards(green, weights, basis, block_layer, pot, dop):
    layers, rows, depth = pot.shape
    e, s = lax.axis_index("energy"), lax.axis_index("space")
    ne, ns = lax.axis_size("energy"), lax.axis_size("space")
    functions = basis[0]
    size = functions.shape[0]
    energies = green.shape[0]
    wide = rows + 8
    block = (layers, rows, depth)
    facts = [e % 2 == 0, block_layer[0], s * layers, e < ne - 1, e > 0, 0, 0, 0]
    place = jnp.broadcast_to(jnp.stack([jnp.asarray(f, F32) for f in facts])[:, None], (8, depth))

    packed_shape = (ne, size + 16, size // 2)
    (copies,) = kernel_call(pack_kernel, (packed_shape, BF16), spaces="vv", room=60)(
        weights[None], green.reshape(energies, size, size)
    )
    even = e % 2 == 0
    pairs = [(i, i ^ 1) for i in range(ne)]
    across = [(i, i + 1) for i in range(1, ne - 1, 2)]
    across = across + [(target, source) for source, target in across]

    late_basis, late_pot, late_dop, copies = lax.optimization_barrier((basis, pot, dop, copies))
    base = late_dop - 6.0 * late_pot + neighbours_in_block(late_pot)
    fields = jnp.concatenate([base, late_pot], axis=0)
    lines = jnp.concatenate([late_basis[0], *in_three(fields)], axis=0)
    lines = jnp.transpose(lines, (1, 0, 2))
    front, back = lines[:HALO], lines[-HALO:]
    pair = lax.ppermute(jnp.where(even, back, front), "energy", pairs)
    outer = lax.ppermute(jnp.where(even, front, back), "energy", across)

    (density,) = kernel_call(
        unpack_kernel,
        ((size, size), BF16),
        spaces="v",
        cost=pl.CostEstimate(flops=10**10, bytes_accessed=10**6, transcendentals=0),
    )(gathered(copies, "energy"))
    applied = jnp.einsum("ij,jyz->iyz", density, functions, preferred_element_type=F32)
    charge_block = jnp.sum(functions * applied, axis=0)

    def from_lines(received, density):
        values = received[:, :size]
        applied = jnp.einsum("ij,yjz->yiz", density, values, preferred_element_type=F32)
        pieces = jnp.split(received[:, size:].astype(F32), 3, axis=1)
        around = jnp.transpose(pieces[0] + pieces[1] + pieces[2], (1, 0, 2))
        return around, jnp.sum(values * applied, axis=1)

    outer, outer_density, charge_block = lax.optimization_barrier((outer, density, charge_block))
    outer_fields, outer_charge = from_lines(outer, outer_density)
    pair, pair_density, outer_charge = lax.optimization_barrier((pair, density, outer_charge))
    pair_fields, pair_charge = from_lines(pair, pair_density)
    message = ((HALO + 2, wide, depth), F32)
    up, down, own = kernel_call(
        edges_kernel, message, message, ((wide, depth), F32), spaces="vvvvvvvv"
    )(
        place,
        base,
        pot,
        charge_block,
        pair_fields,
        pair_charge,
        outer_fields,
        outer_charge,
    )
    lowest = moved(own, "space", 2)
    low = moved(up, "space", 1)
    high = moved(down, "space", -1)

    (part,) = kernel_call(
        arrived_kernel,
        ((layers + 2 * HALO, wide, depth), F32),
        spaces="vvvv",
        cost=pl.CostEstimate(flops=8 * 10**9, bytes_accessed=10**6, transcendentals=0),
    )(place, up, lowest, low)
    field, four = (block, F32), ((4, rows, depth), F32)
    w, mass, n2, handed, mine, copies = kernel_call(
        powers_kernel,
        ((3,) + block, F32),
        field,
        field,
        four,
        four,
        ((ns, 128), F32),
        spaces="vvvvvvv",
    )(place, up, down, part, low, high, pot)
    row = jnp.sum(gathered(copies, "space"), axis=0)
    theirs = moved(handed, "space", -1)
    (parts,) = kernel_call(
        onsite_kernel,
        ((8, size), F32),
        spaces="vvv",
        scratch=[pltpu.VMEM((size, 16 * rows), F32)],
        cost=pl.CostEstimate(
            flops=2 * 256 * size * rows * depth, bytes_accessed=2 * size * rows * depth, transcendentals=0
        ),
    )(basis, mine, theirs)
    row = jnp.pad(row[None], ((4, 3), (0, size - 128)))
    parts = parts + row
    parts = gathered(jnp.broadcast_to(parts[None], (ne,) + parts.shape), "energy")
    potential, residual, onsite = kernel_call(
        finish_kernel, field, field, ((1, size), F32), spaces="vvvvv"
    )(parts, w, mass, n2, pot)
    return (potential, residual, onsite)


def solution(mesh):
    in_specs = (
        P("energy", "space", None, None),
        P("energy"),
        P("space", None, "energy", None),
        P("space"),
        P("space", "energy", None),
        P("space", "energy", None),
    )
    out_specs = (P("space", "energy", None), P("space", "energy", None), P("space", None))
    return jax.shard_map(shards, mesh=mesh, in_specs=in_specs, out_specs=out_specs, check_vma=False)
```
